32 devices in a mesh: dp: 8 (over z, y), blk: 4 (over x, core).
Axes of the slice: x: 2, y: 2, z: 4, core: 2. Of those that a mesh axis runs over, the one named last changes fastest.
Arguments:
- tokens: bfloat16 [4, 8, 512, 768], P(None, 'dp', 'blk'), may hold values from -6 to 6
- document_lengths: int32 [4, 8, 4], P(None, 'dp'), may hold values from 1 to 512, as said below
- joint_weight: bfloat16 [768, 2304], P(('dp', 'blk')), may hold values from -0.21875 to 0.21875
- joint_bias: bfloat16 [2304], P(('dp', 'blk')), may hold values from -4 to 4
- output_weight: bfloat16 [768, 768], P(('dp', 'blk')), may hold values from -1.75 to 1.75
- output_bias: bfloat16 [768], P(('dp', 'blk')), may hold values from -4 to 4
- first_gain: bfloat16 [768], P(('dp', 'blk')), may hold values from 0.5 to 1.5
- first_shift: bfloat16 [768], P(('dp', 'blk')), may hold values from -4 to 4
- expand_weight: bfloat16 [768, 3072], P(('dp', 'blk')), may hold values from -0.21875 to 0.21875
- expand_bias: bfloat16 [3072], P(('dp', 'blk')), may hold values from -4 to 4
- reduce_weight: bfloat16 [3072, 768], P(('dp', 'blk')), may hold values from -0.21875 to 0.21875
- reduce_bias: bfloat16 [768], P(('dp', 'blk')), may hold values from -4 to 4
- second_gain: bfloat16 [768], P(('dp', 'blk')), may hold values from 0.5 to 1.5
- second_shift: bfloat16 [768], P(('dp', 'blk')), may hold values from -4 to 4
- cotangent: bfloat16 [4, 8, 512, 768], P(None, 'dp', 'blk'), may hold values from -6 to 6
Outputs:
- layer_output: bfloat16 [4, 8, 512, 768], P(None, 'dp', 'blk')
- input_gradient: float32 [4, 8, 512, 768], P(None, 'dp', 'blk')
- joint_weight_gradient: float32 [768, 2304], P(('dp', 'blk'))
- joint_bias_gradient: float32 [2304], P(('dp', 'blk'))
- output_weight_gradient: float32 [768, 768], P(('dp', 'blk'))
- output_bias_gradient: float32 [768], P(('dp', 'blk'))
- first_gain_gradient: float32 [768], P(('dp', 'blk'))
- first_shift_gradient: float32 [768], P(('dp', 'blk'))
- expand_weight_gradient: float32 [768, 3072], P(('dp', 'blk'))
- expand_bias_gradient: float32 [3072], P(('dp', 'blk'))
- reduce_weight_gradient: float32 [3072, 768], P(('dp', 'blk'))
- reduce_bias_gradient: float32 [768], P(('dp', 'blk'))
- second_gain_gradient: float32 [768], P(('dp', 'blk'))
- second_shift_gradient: float32 [768], P(('dp', 'blk'))
The draws below stay inside these ranges and needn't reach their ends.
Inputs may be any that keep to these rules, and one draw needn't show every extreme that they name: `document_lengths`: A pack's 4 lengths sum to at most 512; the positions after their sum are padding, which attends only to padding.
All inputs are finite; a program needn't handle non-finite values.
Results may differ from the reference program's by a relative error of at most 0.019.
Values may be sent and summed in bfloat16 or wider, within the bound.
A program may use at most 256 MiB of HBM per device.

```python
import math
import jax
import jax.numpy as jnp
from jax import lax

D = 768
H = 12
HD = 64
FF = 3072
SHARD = 128
MB = 4
DOCS = 4
GROUPS = 8
PACK = 512


def draw_document_lengths(key, part):
    key = jax.random.fold_in(key, 11)
    first_key, finish_key, third_key, fourth_key = jax.random.split(key, 4)
    shape = (MB, GROUPS)
    first = jax.random.randint(first_key, shape, 1, SHARD)
    finish = jax.random.randint(finish_key, shape, PACK - SHARD + 1, PACK - 1)
    tail_rows = PACK - finish
    third = 1 + jax.random.randint(third_key, shape, 0, 1 << 20) % (tail_rows - 1)
    remaining = tail_rows - third
    fourth = 1 + jax.random.randint(fourth_key, shape, 0, 1 << 20) % remaining
    second = finish - first
    return jnp.stack([first, second, third, fourth], axis=-1).astype(jnp.int32)


def shard_levels(key, shape, cuts, least, high):
    level = 1.0
    for axis_at, blocks in cuts:
        steps = jax.random.uniform(jax.random.fold_in(jax.random.fold_in(key, 6), axis_at), (blocks,), jnp.float32, least / len(cuts), high / len(cuts))
        level = level * jnp.repeat(jnp.exp(steps), shape[axis_at] // blocks).reshape((-1,) + (1,) * (len(shape) - 1 - axis_at))
    return level


def centred(key, extent, deviation, most, cuts=(), kind=jnp.bfloat16):
    loudness = shard_levels(key, extent, cuts, -0.22, 0.18) if cuts else 1.0
    drawn = jax.random.normal(key, extent, jnp.float32) * deviation * loudness
    return jnp.minimum(jnp.maximum(drawn, -most), most).astype(kind)


def setup_inputs(seed: int = 0) -> dict:
    streams_of = jax.random.split(jax.random.key(seed), 16)
    return {
        "tokens": centred(streams_of[0], (MB, GROUPS, PACK, D), 1.0, 6.0, ((1, 8), (2, 4))),
        "document_lengths": draw_document_lengths(jax.random.fold_in(streams_of[15], 71), 0),
        "joint_weight": centred(streams_of[2], (D, 3 * D), D ** -0.5, 0.21875, ((0, 32),)),
        "joint_bias": centred(streams_of[3], (3 * D,), 0.3, 4.0, ((0, 32),)),
        "output_weight": centred(streams_of[4], (D, D), (D // 64) ** -0.5, 1.75, ((0, 32),)),
        "output_bias": centred(streams_of[5], (D,), 0.3, 4.0, ((0, 32),)),
        "first_gain": jnp.clip(1.0 + 0.1 * jax.random.normal(streams_of[6], (D,), jnp.float32), 0.5, 1.5).astype(jnp.bfloat16),
        "first_shift": centred(streams_of[7], (D,), 0.3, 4.0, ((0, 32),)),
        "expand_weight": centred(streams_of[8], (D, FF), D ** -0.5, 0.21875, ((0, 32),)),
        "expand_bias": centred(streams_of[9], (FF,), 0.3, 4.0, ((0, 32),)),
        "reduce_weight": centred(streams_of[10], (FF, D), (FF // 4) ** -0.5, 0.21875, ((0, 32),)),
        "reduce_bias": centred(streams_of[11], (D,), 0.3, 4.0, ((0, 32),)),
        "second_gain": jnp.clip(1.0 + 0.1 * jax.random.normal(streams_of[12], (D,), jnp.float32), 0.5, 1.5).astype(jnp.bfloat16),
        "second_shift": centred(streams_of[13], (D,), 0.3, 4.0, ((0, 32),)),
        "cotangent": centred(streams_of[14], (MB, GROUPS, PACK, D), 1.0, 6.0, ((1, 8), (2, 4))),
    }


HIGHEST = lax.Precision.HIGHEST
NEGATIVE = -1e+30
EPSILON = 1e-05

@jax.custom_vjp
def low(v):
    return lax.optimization_barrier(v.astype(jnp.bfloat16)).astype(jnp.float32)

@jax.custom_vjp
def low_back(v):
    return v

def low_keep(v):
    return (low(v), None)

def low_pass(kept, grad):
    return (grad,)

def back_keep(v):
    return (v, None)

def back_low(kept, grad):
    return (low(grad),)
low.defvjp(low_keep, low_pass)
low_back.defvjp(back_keep, back_low)

def product(left, right):
    return jnp.dot(left, right, precision=HIGHEST, preferred_element_type=jnp.float32)

def layout(lengths, places):
    doc_ends = jnp.cumsum(lengths).astype(jnp.int32)
    starts = (doc_ends - lengths).astype(jnp.int32)
    segment = lax.optimization_barrier(jnp.sum((places[:, None] >= doc_ends[None, :]).astype(jnp.int32), axis=1)).astype(jnp.int32)
    labels = jnp.arange(lengths.shape[0], dtype=jnp.int32)
    doc_begin = lax.optimization_barrier(jnp.sum(jnp.where(segment[:, None] == labels[None, :], starts[None, :], 0), axis=1)).astype(jnp.int32)
    doc_begin = jnp.where(segment == lengths.shape[0], doc_ends[-1], doc_begin)
    return (segment, (places - doc_begin).astype(jnp.int32))

def rotate(entries, places, direction):
    half_width = HD // 2
    frequency = 10000.0 ** (-jnp.arange(half_width, dtype=jnp.float32) * (2.0 / HD))
    angles = places.astype(jnp.float32)[:, None] * frequency[None, :]
    cosine = jnp.cos(angles)[:, None, :]
    sine_part = direction * jnp.sin(angles)[:, None, :]
    pieces = entries.reshape(entries.shape[0], -1, HD)
    first_half = pieces[..., :half_width]
    second_half = pieces[..., half_width:]
    turned = jnp.concatenate([first_half * cosine - second_half * sine_part, second_half * cosine + first_half * sine_part], axis=-1)
    return turned.reshape(entries.shape)

def normalize(residual, gain_vector, offset):
    centered = residual - lax.optimization_barrier(jnp.mean(residual, axis=-1, keepdims=True))
    inverse_std = lax.rsqrt(lax.optimization_barrier(jnp.mean(centered * centered, axis=-1, keepdims=True)) + EPSILON)
    return centered * inverse_std * gain_vector + offset

def attend(query, key_rows, value_rows, segment):
    pack_rows = query.shape[0]
    tile_rows = math.gcd(pack_rows, 512)
    tile_count = pack_rows // tile_rows
    query_tiles = query.reshape(tile_count, tile_rows, H, HD)
    segment_tiles = segment.reshape(tile_count, tile_rows)
    all_keys = key_rows.reshape(pack_rows, H, HD)
    all_values = value_rows.reshape(pack_rows, H, HD)

    def one_tile(inputs):
        query_tile, segment_tile = inputs
        scores = low_back(jnp.einsum('qhd,khd->hqk', query_tile, all_keys, precision=HIGHEST) * HD ** (-0.5))
        allowed = (segment_tile[:, None] == segment[None, :])[None]
        scores = jnp.where(allowed, scores, NEGATIVE)
        highest = lax.optimization_barrier(jnp.max(scores, axis=-1, keepdims=True))
        weights = jnp.where(allowed, jnp.exp(scores - highest), 0.0)
        probability = low(weights / lax.optimization_barrier(jnp.sum(weights, axis=-1, keepdims=True)))
        blended = jnp.einsum('hqk,khd->qhd', probability, all_values, precision=HIGHEST)
        return blended.reshape(tile_rows, H * HD)
    return lax.map(jax.checkpoint(one_tile), (query_tiles, segment_tiles)).reshape(pack_rows, H * HD)

def layer(tokens, every_weight, segment, places):
    joint_weight, joint_bias, output_weight, output_bias, first_gain, first_shift, expand_weight, expand_bias, reduce_weight, reduce_bias, second_gain, second_shift = every_weight
    width = D
    joint = low_back(product(tokens, joint_weight) + joint_bias)
    query = low(rotate(joint[:, :width], places, 1.0))
    key_rows = low(rotate(joint[:, width:2 * width], places, 1.0))
    value_rows = low(joint[:, 2 * width:])
    attended = low(low_back(attend(query, key_rows, value_rows, segment)))
    branch = low_back(product(attended, output_weight) + output_bias)
    hidden = normalize(tokens + branch, first_gain, first_shift)
    expanded = low_back(product(low(hidden), expand_weight) + expand_bias)
    active = low(jax.nn.gelu(expanded))
    reduced = low_back(product(active, reduce_weight) + reduce_bias)
    return normalize(hidden + reduced, second_gain, second_shift)

def reference(tokens, document_lengths, joint_weight, joint_bias, output_weight, output_bias, first_gain, first_shift, expand_weight, expand_bias, reduce_weight, reduce_bias, second_gain, second_shift, cotangent):
    every_weight = tuple((record_item.astype(jnp.float32) for record_item in (joint_weight, joint_bias, output_weight, output_bias, first_gain, first_shift, expand_weight, expand_bias, reduce_weight, reduce_bias, second_gain, second_shift)))
    flattened_tokens = tokens.reshape(MB * GROUPS, PACK, D)
    flattened_lengths = document_lengths.reshape(MB * GROUPS, DOCS)
    flattened_cotangent = cotangent.reshape(MB * GROUPS, PACK, D)
    places = jnp.arange(PACK, dtype=jnp.int32)

    def step_forward(running_totals, inputs):
        pack_tokens, lengths, pack_cotangent = inputs
        segment, inner_places = layout(lengths, places)

        def forward(token_values, weight_values):
            return layer(token_values, weight_values, segment, inner_places)
        output_value, pullback = jax.vjp(forward, pack_tokens.astype(jnp.float32), every_weight)
        token_grad, weight_grads = pullback(pack_cotangent.astype(jnp.float32))
        running_totals = tuple((earlier + latest for earlier, latest in zip(running_totals, weight_grads)))
        return (running_totals, (output_value.astype(jnp.bfloat16), token_grad))
    blank_documents = tuple((jnp.zeros_like(record_item) for record_item in every_weight))
    running_totals, (layer_results, token_gradient_rows) = lax.scan(step_forward, blank_documents, (flattened_tokens, flattened_lengths, flattened_cotangent))
    return (layer_results.reshape(tokens.shape), token_gradient_rows.reshape(tokens.shape)) + running_totals
```

```python
import functools
import math

import jax
import jax.numpy as jnp
from jax import lax
from jax.experimental import pallas as pl
from jax.experimental.pallas import tpu as pltpu
from jax.sharding import PartitionSpec as P

H = 12
HD = 64
NEGATIVE = -1e30
EPSILON = 1e-05
MESH = pl.DeviceIdType.MESH
BF16 = jnp.bfloat16
F32 = jnp.float32

VECTOR_ROWS = ((0,), (4,), (1, 2, 3), (5, 6, 7))
VECTOR_TILE = (8, 128)


def pack_vectors(vectors):
    rows = []
    for members in VECTOR_ROWS:
        row = jnp.concatenate([vectors[i].astype(F32) for i in members])
        rows.append(jnp.pad(row, (0, VECTOR_TILE[1] - row.shape[0])))
    packed = jnp.stack(rows)
    return jnp.pad(packed, ((0, VECTOR_TILE[0] - packed.shape[0]), (0, 0)))


def unpack_vectors(packed, widths):
    out = [None] * len(widths)
    for row, members in enumerate(VECTOR_ROWS):
        lane = 0
        for i in members:
            out[i] = packed[..., row, lane : lane + widths[i]].reshape(-1)
            lane += widths[i]
    return out


def place():
    dp = lax.axis_index("dp")
    blk = lax.axis_index("blk")
    return dp // 2, dp % 2, blk // 2, blk % 2


def device(z, y, x, c):
    return (z * 2 + y, x * 2 + c)


def greet(peers):
    barrier = pltpu.get_barrier_semaphore()
    for peer in peers:
        pl.semaphore_signal(barrier, inc=1, device_id=peer, device_id_type=MESH)
    pl.semaphore_wait(barrier, len(peers))


def neighbours(zs):
    z, y, x, c = place()
    sib = device(z, y, x, 1 - c)
    xpeer = device(z, y, 1 - x, c)
    ypeer = device(z, 1 - y, x, c)
    zpeers = [device((z + k) % zs, y, x, c) for k in range(1, zs)]
    return sib, xpeer, ypeer, zpeers


def remote(src, dst, sems, index, peer):
    send, recv = sems
    return pltpu.make_async_remote_copy(
        src_ref=src,
        dst_ref=dst,
        send_sem=send.at[index],
        recv_sem=recv.at[index],
        device_id=peer,
        device_id_type=MESH,
    )


def pick(c, first, second):
    return first + c * (second - first)


def gather_kernel(
    zs,
    jw,
    ow,
    ew,
    rw,
    vec,
    tok,
    J,
    O,
    E,
    R,
    V,
    T,
    stage_j,
    stage_o,
    stage_e,
    pair_j,
    pair_o,
    pair_e,
    pair_send,
    pair_recv,
    send,
    recv,
    tok_send,
    tok_recv,
):
    z, y, x, c = place()
    sib, xpeer, ypeer, zpeers = neighbours(zs)
    greet([sib, xpeer, ypeer] + zpeers)
    blk = x * 2 + c
    T[blk] = tok[...]
    tok_sems = (tok_send, tok_recv)
    tok_x = remote(T.at[blk], T.at[blk], tok_sems, 0, xpeer)
    tok_s = remote(T.at[blk], T.at[blk], tok_sems, 1, sib)
    tok_x.start()
    tok_s.start()

    pair_sems = (pair_send, pair_recv)
    pairs = []
    for i, (w, stage, pair) in enumerate(
        ((jw, stage_j, pair_j), (ow, stage_o, pair_o), (ew, stage_e, pair_e))
    ):
        half = stage.shape[2]
        stage[0] = w[:, :half].astype(F32)
        stage[1] = w[:, half:].astype(F32)
        copy = remote(stage.at[1 - c], pair, pair_sems, i, sib)
        copy.start()
        pairs.append(copy)
    R[z, y, x, c] = rw[...]
    V[z, y, x, c] = vec[...]

    paired = ((J, stage_j, pair_j), (O, stage_o, pair_o), (E, stage_e, pair_e))
    items = (
        (V, False),
        (J, True),
        (O, True),
        (E, True),
        (R, False),
    )

    def block(ref, halves, bz, by, bx, bc):
        return ref.at[bc, bz, by, bx] if halves else ref.at[bz, by, bx, bc]

    def column(ref, halves, by, bx, bc):
        return ref.at[bc, :, by, bx] if halves else ref.at[:, by, bx, bc]

    sems = (send, recv)
    z_copies, col_copies, forwards, shares = [], [], [], []

    def start_z(i):
        ref, halves = items[i]
        own = block(ref, halves, z, y, x, c)
        copies = [remote(own, own, sems, (i, k), peer) for k, peer in enumerate(zpeers)]
        for copy in copies:
            copy.start()
        z_copies.append(copies)

    start_z(0)
    for n, (W, stage, pair) in enumerate(paired):
        pairs[n].wait_recv()
        mine = stage[c]
        other = pair[...]
        first = jnp.where(c == 0, mine, other)
        second = jnp.where(c == 0, other, mine)
        W[c, z, y, x] = jnp.concatenate([first, second], axis=0).astype(BF16)
        start_z(n + 1)
    start_z(4)

    base = zs - 1
    forward_to = tuple(pick(c, a, b) for a, b in zip(xpeer, ypeer))
    fy, fx = pick(c, 1 - y, y), pick(c, x, 1 - x)
    ry, rx = 1 - y, 1 - x
    for i, (ref, halves) in enumerate(items):
        for copy in z_copies[i]:
            copy.wait_recv()
        own = column(ref, halves, y, x, c)
        to_x = remote(own, own, sems, (i, base), xpeer)
        to_y = remote(own, own, sems, (i, base + 1), ypeer)
        to_sib = remote(own, own, sems, (i, base + 3), sib)
        to_x.start()
        to_y.start()
        to_sib.start()
        col_copies.append((to_x, to_y, to_sib))
    for i, (ref, halves) in enumerate(items):
        to_x, to_y, to_sib = col_copies[i]
        to_x.wait_recv()
        to_y.wait_recv()
        got = column(ref, halves, fy, fx, c)
        forward = remote(got, got, sems, (i, base + 2), forward_to)
        forward.start()
        share_x = column(ref, halves, y, 1 - x, c)
        share_y = column(ref, halves, 1 - y, x, c)
        sx = remote(share_x, share_x, sems, (i, base + 4), sib)
        sy = remote(share_y, share_y, sems, (i, base + 5), sib)
        sx.start()
        sy.start()
        forwards.append((forward, sx, sy))
    tok_x.wait_recv()
    other_x = (1 - x) * 2 + c
    tok_f = remote(T.at[other_x], T.at[other_x], tok_sems, 2, sib)
    tok_f.start()
    for i, (ref, halves) in enumerate(items):
        forward, sx, sy = forwards[i]
        forward.wait_recv()
        share_d = column(ref, halves, ry, rx, c)
        sd = remote(share_d, share_d, sems, (i, base + 6), sib)
        sd.start()
        shares.append(sd)
    for i in range(len(items)):
        for copy in (col_copies[i][2], forwards[i][1], forwards[i][2], shares[i]):
            copy.wait_recv()
    tok_s.wait_recv()
    tok_f.wait_recv()
    for copy in pairs + [tok_x, tok_s, tok_f]:
        copy.wait_send()
    for i in range(len(items)):
        for copy in tuple(z_copies[i]) + col_copies[i] + forwards[i] + (shares[i],):
            copy.wait_send()


def gather(zs, weights, vec, tok):
    jw, ow, ew, rw = weights
    vmem = pl.BlockSpec(memory_space=pltpu.VMEM)

    def halves(w):
        return (2, zs, 2, 2, 2 * w.shape[0], w.shape[1] // 2)

    shapes = [jax.ShapeDtypeStruct(halves(w), BF16) for w in (jw, ow, ew)] + [
        jax.ShapeDtypeStruct((zs, 2, 2, 2) + rw.shape, BF16),
        jax.ShapeDtypeStruct((zs, 2, 2, 2) + vec.shape, F32),
        jax.ShapeDtypeStruct((4,) + tok.shape, BF16),
    ]
    stages = [pltpu.VMEM((2, w.shape[0], w.shape[1] // 2), F32) for w in (jw, ow, ew)]
    pairs = [pltpu.VMEM((w.shape[0], w.shape[1] // 2), F32) for w in (jw, ow, ew)]
    dma = pltpu.SemaphoreType.DMA
    return pl.pallas_call(
        functools.partial(gather_kernel, zs),
        out_shape=shapes,
        in_specs=[vmem] * 6,
        out_specs=[vmem] * 6,
        scratch_shapes=stages
        + pairs
        + [dma((3,)), dma((3,)), dma((5, zs + 6)), dma((5, zs + 6)), dma((3,)), dma((3,))],
        compiler_params=pltpu.CompilerParams(
            collective_id=0, has_side_effects=True, vmem_limit_bytes=48 << 20
        ),
    )(jw, ow, ew, rw, vec, tok)


def scatter_kernel(
    zs,
    GJ,
    GO,
    GE,
    GR,
    GV,
    DX,
    base_x,
    gj,
    go,
    ge,
    gr,
    gv,
    gx,
    *scratch,
):
    z, y, x, c = place()
    sib, xpeer, ypeer, zpeers = neighbours(zs)
    greet([sib, xpeer, ypeer] + zpeers)
    sums, diags, near2, near3, zbufs = (scratch[5 * i : 5 * i + 5] for i in range(5))
    fin_j, fin_o, fin_e, got_j, got_o, got_e, sx, rx_buf, send, recv, dx_send, dx_recv = scratch[25:]
    sems = (send, recv)
    items = ((GR, False), (GE, True), (GO, True), (GJ, True), (GV, False))
    over3 = tuple(pick(c, a, b) for a, b in zip(xpeer, ypeer))
    over2 = tuple(pick(c, a, b) for a, b in zip(ypeer, xpeer))
    y3, x3 = pick(c, y, 1 - y), pick(c, 1 - x, x)
    y2, x2 = pick(c, 1 - y, y), pick(c, x, 1 - x)

    first = []
    for i, (ref, halves) in enumerate(items):
        src = ref.at[1 - c] if halves else ref.at[:, :, :, 1 - c]
        copy = remote(src, sums[i], sems, (i, 0), sib)
        copy.start()
        first.append(copy)
    dx_sems = (dx_send, dx_recv)
    dx_sib = remote(DX.at[:, 1 - c], sx, dx_sems, 0, sib)
    dx_sib.start()

    second = []
    for i, (ref, halves) in enumerate(items):
        first[i].wait_recv()

        def add_block(n, carry, ref=ref, halves=halves, i=i):
            az, ay, ax = n // 4, (n // 2) % 2, n % 2
            own = ref[c, az, ay, ax] if halves else ref[az, ay, ax, c]
            total = own.astype(F32) + sums[i][az, ay, ax].astype(F32)
            sums[i][az, ay, ax] = total.astype(sums[i].dtype)
            return carry

        lax.fori_loop(0, zs * 4, add_block, 0)
        diag = remote(sums[i].at[:, 1 - y, 1 - x], diags[i], sems, (i, 1), over3)
        near = remote(sums[i].at[:, y3, x3], near3[i], sems, (i, 2), over3)
        diag.start()
        near.start()
        second.append((diag, near))
    dx_sib.wait_recv()
    for n in range(2):
        sx[n] = (sx[n].astype(F32) + DX[n, c].astype(F32)).astype(BF16)
    dx_x = remote(sx.at[1 - x], rx_buf, dx_sems, 1, xpeer)
    dx_x.start()

    third = []
    for i in range(len(items)):
        second[i][0].wait_recv()

        def add_diag(n, carry, i=i):
            total = sums[i][n, y2, x2].astype(F32) + diags[i][n].astype(F32)
            sums[i][n, y2, x2] = total.astype(sums[i].dtype)
            return carry

        lax.fori_loop(0, zs, add_diag, 0)
        copy = remote(sums[i].at[:, y2, x2], near2[i], sems, (i, 3), over2)
        copy.start()
        third.append(copy)

    fourth = []
    for i in range(len(items)):
        second[i][1].wait_recv()
        third[i].wait_recv()

        def add_near(n, carry, i=i):
            total = (
                sums[i][n, y, x].astype(F32) + near3[i][n].astype(F32) + near2[i][n].astype(F32)
            )
            sums[i][n, y, x] = total.astype(sums[i].dtype)
            return carry

        lax.fori_loop(0, zs, add_near, 0)
        copies = []
        for k, peer in enumerate(zpeers):
            copy = remote(
                sums[i].at[(z + k + 1) % zs, y, x], zbufs[i].at[k], sems, (i, 4 + k), peer
            )
            copy.start()
            copies.append(copy)
        fourth.append(copies)

    fins = (None, fin_e, fin_o, fin_j, None)
    gots = (None, got_e, got_o, got_j, None)
    outs = (gr, ge, go, gj, gv)
    last = []
    for i in range(len(items)):
        for copy in fourth[i]:
            copy.wait_recv()
        total = sums[i][z, y, x].astype(F32)
        for k in range(zs - 1):
            total = total + zbufs[i][k].astype(F32)
        if fins[i] is None:
            outs[i][...] = total
            last.append(None)
        else:
            rows = fins[i].shape[1]
            fins[i][0] = total[:rows]
            fins[i][1] = total[rows:]
            copy = remote(fins[i].at[1 - c], gots[i], sems, (i, 3 + zs), sib)
            copy.start()
            last.append(copy)
    dx_x.wait_recv()
    gx[...] = base_x[...] + sx[x].astype(F32) + rx_buf[...].astype(F32)
    for i in range(len(items)):
        if fins[i] is None:
            continue
        last[i].wait_recv()
        width = fins[i].shape[2]
        mine = fins[i][c]
        other = gots[i][...]
        outs[i][:, :width] = jnp.where(c == 0, mine, other)
        outs[i][:, width:] = jnp.where(c == 0, other, mine)
    dx_sib.wait_send()
    dx_x.wait_send()
    for i in range(len(items)):
        for copy in (first[i],) + second[i] + (third[i],) + tuple(fourth[i]):
            copy.wait_send()
        if last[i] is not None:
            last[i].wait_send()


def scatter(zs, GJ, GO, GE, GR, GV, DX, base_x):
    def split(g):
        return g.reshape(2, zs, 2, 2, g.shape[1] // (4 * zs), g.shape[2])

    GJ, GO, GE = split(GJ), split(GO), split(GE)
    GR = GR.reshape(zs, 2, 2, 2, GR.shape[0] // (8 * zs), GR.shape[1])
    GV = GV.reshape((zs, 2, 2, 2) + GV.shape[1:])
    DX = DX.reshape((2, 2) + DX.shape[1:])
    vmem = pl.BlockSpec(memory_space=pltpu.VMEM)
    blocks = [(a.shape[4:], a.dtype) for a in (GR, GE, GO, GJ, GV)]

    def buffers(lead):
        return [pltpu.VMEM(lead + shape, dtype) for shape, dtype in blocks]

    pairs = [(g.shape[4] // 2, g.shape[5]) for g in (GJ, GO, GE)]
    dma = pltpu.SemaphoreType.DMA
    scratch = (
        buffers((zs, 2, 2))
        + buffers((zs,))
        + buffers((zs,))
        + buffers((zs,))
        + buffers((zs - 1,))
        + [pltpu.VMEM((2,) + p, F32) for p in pairs]
        + [pltpu.VMEM(p, F32) for p in pairs]
        + [pltpu.VMEM((2,) + DX.shape[2:], BF16), pltpu.VMEM(DX.shape[2:], BF16)]
        + [dma((5, zs + 4)), dma((5, zs + 4)), dma((2,)), dma((2,))]
    )
    shapes = [jax.ShapeDtypeStruct((p[0], 2 * p[1]), F32) for p in pairs] + [
        jax.ShapeDtypeStruct(GR.shape[4:], F32),
        jax.ShapeDtypeStruct(GV.shape[4:], F32),
        jax.ShapeDtypeStruct(base_x.shape, F32),
    ]
    return pl.pallas_call(
        functools.partial(scatter_kernel, zs),
        out_shape=shapes,
        in_specs=[vmem] * 7,
        out_specs=[vmem] * 6,
        scratch_shapes=scratch,
        compiler_params=pltpu.CompilerParams(
            collective_id=1, has_side_effects=True, vmem_limit_bytes=60 << 20
        ),
    )(GJ, GO, GE, GR, GV, DX, base_x)


def layout(lengths, places):
    doc_ends = jnp.cumsum(lengths)
    starts = doc_ends - lengths
    segment = jnp.sum((places[:, None] >= doc_ends[None, :]).astype(jnp.int32), axis=1)
    labels = jnp.arange(lengths.shape[0], dtype=jnp.int32)
    doc_begin = jnp.sum(jnp.where(segment[:, None] == labels[None, :], starts[None, :], 0), axis=1)
    doc_begin = jnp.where(segment == lengths.shape[0], doc_ends[-1], doc_begin)
    return (segment, places - doc_begin)


def rotate(entries, angles, direction):
    half_width = HD // 2
    cosine = jnp.cos(angles)[:, :, None, :]
    sine_part = direction * jnp.sin(angles)[:, :, None, :]
    pieces = entries.reshape(entries.shape[0], entries.shape[1], -1, HD)
    first_half = pieces[..., :half_width]
    second_half = pieces[..., half_width:]
    turned = jnp.concatenate(
        [
            first_half * cosine - second_half * sine_part,
            second_half * cosine + first_half * sine_part,
        ],
        axis=-1,
    )
    return turned.reshape(entries.shape)


def normalize(residual, gain_vector, offset):
    centered = residual - jnp.mean(residual, axis=-1, keepdims=True)
    inverse_std = lax.rsqrt(jnp.mean(centered * centered, axis=-1, keepdims=True) + EPSILON)
    return centered * inverse_std * gain_vector + offset


def contract_rows(left, right):
    return lax.dot_general(
        left, right, (((0,), (0,)), ((), ())), preferred_element_type=F32
    )


def times_transposed(left, right):
    return lax.dot_general(
        left, right, (((1,), (1,)), ((), ())), preferred_element_type=F32
    )


def column_sum(values):
    return jnp.sum(values.astype(F32), axis=0)


def per_device(
    mesh_shape,
    tokens,
    document_lengths,
    joint_weight,
    joint_bias,
    output_weight,
    output_bias,
    first_gain,
    first_shift,
    expand_weight,
    expand_bias,
    reduce_weight,
    reduce_bias,
    second_gain,
    second_shift,
    cotangent,
):
    dp_size, blk_size = mesh_shape
    micro, _, shard_rows, width = tokens.shape
    own = micro * shard_rows
    pack_rows = shard_rows * blk_size
    vectors = (
        joint_bias,
        output_bias,
        first_gain,
        first_shift,
        expand_bias,
        reduce_bias,
        second_gain,
        second_shift,
    )
    widths = [v.shape[0] for v in vectors]
    use_kernels = (
        blk_size == 4 and dp_size % 2 == 0 and (2 * joint_weight.shape[0]) % 16 == 0
    )
    zs = dp_size // 2
    axes = ("dp", "blk")
    tokens_own = tokens[:, 0]
    if use_kernels:
        J, O, E, R, V, T = gather(
            zs,
            (joint_weight, output_weight, expand_weight, reduce_weight),
            pack_vectors(vectors),
            tokens_own,
        )

        def whole(w):
            flat = w.reshape(2, -1, w.shape[-1])
            return jnp.concatenate([flat[0], flat[1]], axis=1)

        joint_full, output_full, expand_full = whole(J), whole(O), whole(E)
        reduce_full = R.reshape(-1, R.shape[-1])
        vector_full = unpack_vectors(V.reshape((-1,) + VECTOR_TILE), widths)
        pack = T
    else:
        joint_full, output_full, expand_full, reduce_full = (
            lax.all_gather(w, axes, axis=0, tiled=True)
            for w in (joint_weight, output_weight, expand_weight, reduce_weight)
        )
        packed = lax.all_gather(jnp.concatenate(vectors), axes, axis=0)
        cuts = [sum(widths[: i + 1]) for i in range(len(widths) - 1)]
        vector_full = [
            v.reshape(-1).astype(F32) for v in jnp.split(packed, cuts, axis=1)
        ]
        pack = lax.all_gather(tokens_own, "blk", axis=0)
    joint_b, output_b, gain1, shift1, expand_b, reduce_b, gain2, shift2 = vector_full

    pack_tokens = pack.transpose(1, 0, 2, 3).reshape(micro, pack_rows, width)
    lengths = document_lengths[:, 0]
    all_places = jnp.arange(pack_rows, dtype=jnp.int32)
    own_start = lax.axis_index("blk") * shard_rows
    key_segment, key_inner = jax.vmap(layout, (0, None))(lengths, all_places)
    segment = lax.dynamic_slice_in_dim(key_segment, own_start, shard_rows, 1)
    inner = lax.dynamic_slice_in_dim(key_inner, own_start, shard_rows, 1)
    frequency = 10000.0 ** (-jnp.arange(HD // 2, dtype=F32) * (2.0 / HD))
    key_angles = key_inner.astype(F32)[..., None] * frequency
    query_angles = inner.astype(F32)[..., None] * frequency
    score_scale = HD ** (-0.5)

    token_low = tokens_own.reshape(own, width)
    token_float = token_low.astype(F32)
    query_weight, pair_weight = joint_full[:, :width], joint_full[:, width:]
    query = jnp.dot(token_low, query_weight, preferred_element_type=F32) + joint_b[:width]
    query = rotate(query.reshape(micro, shard_rows, width), query_angles, 1.0).astype(BF16)
    pair = (
        jnp.dot(
            pack_tokens.reshape(micro * pack_rows, width),
            pair_weight,
            preferred_element_type=F32,
        )
        + joint_b[width:]
    ).reshape(micro, pack_rows, 2 * width)
    keys = rotate(pair[..., :width], key_angles, 1.0).astype(BF16)
    values = pair[..., width:].astype(BF16)
    query_heads = query.reshape(micro, shard_rows, H, HD)
    key_heads = keys.reshape(micro, pack_rows, H, HD)
    value_heads = values.reshape(micro, pack_rows, H, HD)
    allowed = (segment[:, :, None] == key_segment[:, None, :])[:, None]
    scores = (
        jnp.einsum("mqhd,mkhd->mhqk", query_heads, key_heads, preferred_element_type=F32)
        * score_scale
    )
    scores = jnp.where(allowed, scores, NEGATIVE)
    highest = jnp.max(scores, axis=-1, keepdims=True)
    weights = jnp.where(allowed, jnp.exp(scores - highest), 0.0)
    probability = weights / jnp.sum(weights, axis=-1, keepdims=True)
    probability_low = probability.astype(BF16)
    attended = (
        jnp.einsum("mhqk,mkhd->mqhd", probability_low, value_heads, preferred_element_type=F32)
        .reshape(own, width)
        .astype(BF16)
    )
    branch = jnp.dot(attended, output_full, preferred_element_type=F32) + output_b
    hidden, first_pullback = jax.vjp(normalize, token_float + branch, gain1, shift1)
    hidden_low = hidden.astype(BF16)
    expanded = jnp.dot(hidden_low, expand_full, preferred_element_type=F32) + expand_b
    active_float, gelu_pullback = jax.vjp(jax.nn.gelu, expanded)
    active = active_float.astype(BF16)
    reduced = jnp.dot(active, reduce_full, preferred_element_type=F32) + reduce_b
    result, second_pullback = jax.vjp(normalize, hidden + reduced, gain2, shift2)
    layer_output = result.astype(BF16).reshape(tokens.shape)

    second_residual, second_gain_grad, second_shift_grad = second_pullback(
        cotangent[:, 0].reshape(own, width).astype(F32)
    )
    reduced_grad = second_residual.astype(BF16)
    reduce_weight_grad = contract_rows(active, reduced_grad)
    reduce_bias_grad = column_sum(reduced_grad)
    (expanded_float,) = gelu_pullback(times_transposed(reduced_grad, reduce_full))
    expanded_grad = expanded_float.astype(BF16)
    expand_bias_grad = column_sum(expanded_grad)
    hidden_grad = second_residual + times_transposed(expanded_grad, expand_full)
    first_residual, first_gain_grad, first_shift_grad = first_pullback(hidden_grad)
    branch_grad = first_residual.astype(BF16)
    output_bias_grad = column_sum(branch_grad)
    attended_grad = times_transposed(branch_grad, output_full).astype(BF16)
    attended_heads = attended_grad.reshape(micro, shard_rows, H, HD)
    prob_grad = jnp.einsum(
        "mqhd,mkhd->mhqk", attended_heads, value_heads, preferred_element_type=F32
    )
    delta = jnp.sum(probability * prob_grad, axis=-1, keepdims=True)
    score_grad = (probability * (prob_grad - delta)).astype(BF16)
    query_grad = (
        jnp.einsum("mhqk,mkhd->mqhd", score_grad, key_heads, preferred_element_type=F32)
        * score_scale
    ).reshape(micro, shard_rows, width)
    key_grad = (
        jnp.einsum("mhqk,mqhd->mkhd", score_grad, query_heads, preferred_element_type=F32)
        * score_scale
    ).reshape(micro, pack_rows, width)
    value_grad = jnp.einsum(
        "mhqk,mqhd->mkhd", probability_low, attended_heads, preferred_element_type=F32
    ).reshape(micro, pack_rows, width)
    query_back = rotate(query_grad, query_angles, -1.0).reshape(own, width).astype(BF16)
    key_back = rotate(key_grad, key_angles, -1.0)
    pair_back = (
        jnp.concatenate([key_back, value_grad], axis=-1)
        .astype(BF16)
        .reshape(micro * pack_rows, 2 * width)
    )
    joint_bias_grad = jnp.concatenate([column_sum(query_back), column_sum(pair_back)])
    pack_flat = pack_tokens.reshape(micro * pack_rows, width)
    near_gradient = first_residual + times_transposed(query_back, query_weight)
    far_gradient = (
        times_transposed(pair_back, pair_weight)
        .astype(BF16)
        .reshape(micro, blk_size, shard_rows, width)
        .transpose(1, 0, 2, 3)
    )
    near_gradient = near_gradient.reshape(tokens_own.shape)
    vector_grads = (
        joint_bias_grad,
        output_bias_grad,
        first_gain_grad,
        first_shift_grad,
        expand_bias_grad,
        reduce_bias_grad,
        second_gain_grad,
        second_shift_grad,
    )
    joint_grad = jnp.concatenate(
        [contract_rows(token_low, query_back), contract_rows(pack_flat, pair_back)], axis=1
    )
    output_grad = contract_rows(attended, branch_grad)
    expand_grad = contract_rows(hidden_low, expanded_grad)
    if use_kernels:

        def halves(g):
            half = g.shape[1] // 2
            return jnp.stack([g[:, :half], g[:, half:]]).astype(BF16)

        devices = dp_size * blk_size
        packed = jax.vmap(pack_vectors)([v.reshape(devices, -1) for v in vector_grads])
        gj, go, ge, gr, gv, gx = scatter(
            zs,
            halves(joint_grad),
            halves(output_grad),
            halves(expand_grad),
            reduce_weight_grad.astype(BF16),
            packed,
            far_gradient,
            near_gradient,
        )
        shares = unpack_vectors(gv, widths)
        input_gradient = gx
    else:
        gj, go, ge, gr = (
            lax.psum_scatter(g, axes, scatter_dimension=0, tiled=True)
            for g in (joint_grad, output_grad, expand_grad, reduce_weight_grad)
        )
        devices = dp_size * blk_size
        packed = jnp.concatenate([v.reshape(devices, -1) for v in vector_grads], axis=1)
        summed = lax.psum_scatter(packed, axes, scatter_dimension=0, tiled=True)
        cuts = [sum(widths[: i + 1]) for i in range(len(widths) - 1)]
        shares = [v.reshape(-1) for v in jnp.split(summed, cuts, axis=1)]
        far = lax.psum_scatter(far_gradient, "blk", scatter_dimension=0, tiled=True)
        input_gradient = near_gradient + far[0].astype(F32)
    return (
        layer_output,
        input_gradient[:, None],
        gj,
        shares[0],
        go,
        shares[1],
        shares[2],
        shares[3],
        ge,
        shares[4],
        gr,
        shares[5],
        shares[6],
        shares[7],
    )


def solution(mesh):
    rows = P(("dp", "blk"), None)
    row = P(("dp", "blk"))
    packs = P(None, "dp", "blk", None)
    parameters = (rows, row, rows, row, row, row, rows, row, rows, row, row, row)
    return jax.shard_map(
        functools.partial(per_device, (mesh.shape["dp"], mesh.shape["blk"])),
        mesh=mesh,
        in_specs=(packs, P(None, "dp", None)) + parameters + (packs,),
        out_specs=(packs, packs) + parameters,
        check_vma=False,
    )
```

```python
import functools
import math

import jax
import jax.numpy as jnp
import numpy as np
from jax import lax
from jax.experimental import pallas as pl
from jax.experimental.pallas import tpu as pltpu
from jax.sharding import PartitionSpec as P

H = 12
HD = 64
NEGATIVE = -1e30
EPSILON = 1e-05
MESH = pl.DeviceIdType.MESH
BF16 = jnp.bfloat16
F32 = jnp.float32

VECTOR_ROWS = ((0,), (4,), (1, 2, 3), (5, 6, 7))
VECTOR_TILE = (8, 128)


def pack_vectors(vectors):
    rows = []
    for members in VECTOR_ROWS:
        row = jnp.concatenate([vectors[i].astype(F32) for i in members])
        rows.append(jnp.pad(row, (0, VECTOR_TILE[1] - row.shape[0])))
    packed = jnp.stack(rows)
    return jnp.pad(packed, ((0, VECTOR_TILE[0] - packed.shape[0]), (0, 0)))


def unpack_vectors(packed, widths):
    out = [None] * len(widths)
    for row, members in enumerate(VECTOR_ROWS):
        lane = 0
        for i in members:
            out[i] = packed[..., row, lane : lane + widths[i]].reshape(-1)
            lane += widths[i]
    return out


def place():
    dp = lax.axis_index("dp")
    blk = lax.axis_index("blk")
    return dp // 2, dp % 2, blk // 2, blk % 2


def device(z, y, x, c):
    return (z * 2 + y, x * 2 + c)


def greet(peers):
    barrier = pltpu.get_barrier_semaphore()
    for peer in peers:
        pl.semaphore_signal(barrier, inc=1, device_id=peer, device_id_type=MESH)
    pl.semaphore_wait(barrier, len(peers))


def neighbours(zs):
    z, y, x, c = place()
    sib = device(z, y, x, 1 - c)
    xpeer = device(z, y, 1 - x, c)
    ypeer = device(z, 1 - y, x, c)
    zpeers = [device((z + k) % zs, y, x, c) for k in range(1, zs)]
    return sib, xpeer, ypeer, zpeers


def remote(src, dst, sems, index, peer):
    send, recv = sems
    return pltpu.make_async_remote_copy(
        src_ref=src,
        dst_ref=dst,
        send_sem=send.at[index],
        recv_sem=recv.at[index],
        device_id=peer,
        device_id_type=MESH,
    )


def pick(c, first, second):
    return first + c * (second - first)


class Links:
    def __init__(self, zs):
        self.zs = zs
        self.z, self.y, self.x, self.c = z, y, x, c = place()
        self.sib, self.xpeer, self.ypeer, self.zpeers = neighbours(zs)
        self.mix = (
            tuple(pick(c, a, b) for a, b in zip(self.xpeer, self.ypeer)),
            tuple(pick(c, a, b) for a, b in zip(self.ypeer, self.xpeer)),
            (pick(c, y, 1 - y), pick(c, 1 - x, x)),
            (pick(c, 1 - y, y), pick(c, x, 1 - x)),
        )
        self.over_y = (self.ypeer, self.xpeer, (1 - y, x), (y, 1 - x))


class Again:
    def __init__(self, make):
        self.make = make

    def start(self):
        self.make().start()

    def wait_recv(self):
        self.make().wait_recv()

    def wait_send(self):
        self.make().wait_send()


class Mover:
    def __init__(self, links, sems, row):
        self.l, self.sems, self.row = links, sems, row
        self.started = []

    def send(self, index, src, dst, peer):
        copy = Again(lambda: remote(src(), dst(), self.sems, (self.row, index), peer))
        copy.start()
        self.started.append(copy)
        return copy

    def hand(self, index, ref, peer):
        return self.send(index, ref, ref, peer)

    def drain(self):
        for copy in self.started:
            copy.wait_send()
        self.started = []


class GatherZFirst(Mover):
    def __init__(self, links, sems, row, block, column):
        super().__init__(links, sems, row)
        self.block, self.column = block, column

    def start(self):
        l = self.l
        own = lambda: self.block(l.z, l.y, l.x)
        self.zc = [self.hand(k, own, peer) for k, peer in enumerate(l.zpeers)]

    def columns(self):
        l, b = self.l, self.l.zs - 1
        for copy in self.zc:
            copy.wait_recv()
        own = lambda: self.column(l.y, l.x)
        self.tx = self.hand(b, own, l.xpeer)
        self.ty = self.hand(b + 1, own, l.ypeer)
        self.shares = [self.hand(b + 3, own, l.sib)]

    def forward(self):
        l, b = self.l, self.l.zs - 1
        self.tx.wait_recv()
        self.ty.wait_recv()
        to, _, _, (fy, fx) = l.mix
        self.fw = self.hand(b + 2, lambda: self.column(fy, fx), to)
        self.shares.append(self.hand(b + 4, lambda: self.column(l.y, 1 - l.x), l.sib))
        self.shares.append(self.hand(b + 5, lambda: self.column(1 - l.y, l.x), l.sib))

    def last(self):
        l, b = self.l, self.l.zs - 1
        self.fw.wait_recv()
        self.shares.append(self.hand(b + 6, lambda: self.column(1 - l.y, 1 - l.x), l.sib))

    def finish(self):
        for copy in self.shares:
            copy.wait_recv()


class GatherZLast(Mover):
    def __init__(self, links, sems, row, block, plane):
        super().__init__(links, sems, row)
        self.block, self.plane = block, plane

    def start(self):
        l = self.l
        own = lambda: self.block(l.z, l.y, l.x)
        self.tx = self.hand(0, own, l.xpeer)
        self.ty = self.hand(1, own, l.ypeer)

    def forward(self):
        l = self.l
        self.tx.wait_recv()
        self.ty.wait_recv()
        to, _, _, (fy, fx) = l.mix
        self.fw = self.hand(2, lambda: self.block(l.z, fy, fx), to)

    def planes(self):
        l = self.l
        self.fw.wait_recv()
        own = lambda: self.plane(l.z)
        self.zc = [self.hand(3 + k, own, peer) for k, peer in enumerate(l.zpeers)]
        self.shares = [self.hand(2 + l.zs, own, l.sib)]

    def last(self):
        l = self.l
        for k, copy in enumerate(self.zc):
            copy.wait_recv()
            came = lambda k=k: self.plane((l.z + l.zs - 1 - k) % l.zs)
            self.shares.append(self.hand(3 + l.zs + k, came, l.sib))

    finish = GatherZFirst.finish


def add_into(ref, *others):
    total = ref[...].astype(F32)
    for other in others:
        total = total + other[...].astype(F32)
    ref[...] = total.astype(ref.dtype)


class ScatterZFirst(Mover):
    def __init__(self, links, sems, row, sums, bufs, own, over):
        super().__init__(links, sems, row)
        self.block, self.column = sums
        self.diag, self.n3, self.n2, self.zb = bufs
        self.own = own
        self.over = over

    def add_sib(self, waits):
        l = self.l
        for copy in waits:
            copy.wait_recv()

        def body(n, carry):
            at = (n // 4, (n // 2) % 2, n % 2)
            add_into(self.block(*at), self.own(*at))
            return carry

        lax.fori_loop(0, 4 * l.zs, body, 0)
        peer3, peer2, (y3, x3), (y2, x2) = self.over
        self.c3 = self.send(0, lambda: self.column(1 - l.y, 1 - l.x), lambda: self.diag, peer3)
        self.cn = self.send(1, lambda: self.column(y3, x3), lambda: self.n3, peer3)

    def add_diag(self):
        l = self.l
        peer3, peer2, (y3, x3), (y2, x2) = self.over
        self.c3.wait_recv()

        def body(n, carry):
            add_into(self.block(n, y2, x2), self.diag.at[n])
            return carry

        lax.fori_loop(0, l.zs, body, 0)
        self.c2 = self.send(2, lambda: self.column(y2, x2), lambda: self.n2, peer2)

    def add_near(self):
        l = self.l
        self.cn.wait_recv()
        self.c2.wait_recv()

        def body(n, carry):
            add_into(self.block(n, l.y, l.x), self.n3.at[n], self.n2.at[n])
            return carry

        lax.fori_loop(0, l.zs, body, 0)
        self.zc = [
            self.send(
                3 + k,
                lambda k=k: self.block((l.z + k + 1) % l.zs, l.y, l.x),
                lambda k=k: self.zb.at[k],
                peer,
            )
            for k, peer in enumerate(l.zpeers)
        ]

    def total(self):
        l = self.l
        for copy in self.zc:
            copy.wait_recv()
        total = self.block(l.z, l.y, l.x)[...].astype(F32)
        for k in range(l.zs - 1):
            total = total + self.zb[k].astype(F32)
        return total


class ScatterZLast(Mover):
    def __init__(self, links, sems, row, sums, bufs, own, over):
        super().__init__(links, sems, row)
        self.block, self.plane = sums
        self.diag, self.n3, self.n2, self.zb = bufs
        self.own = own
        self.over = over

    def add_sib(self, waits):
        l = self.l
        for copy in waits:
            copy.wait_recv()

        def body(n, carry):
            at = (n // 4, (n // 2) % 2, n % 2)
            add_into(self.block(*at), self.own(*at))
            return carry

        lax.fori_loop(0, 4 * l.zs, body, 0)
        self.zc = [
            self.send(
                3 + k,
                lambda k=k: self.plane((l.z + k + 1) % l.zs),
                lambda k=k: self.zb.at[k],
                peer,
            )
            for k, peer in enumerate(l.zpeers)
        ]

    def add_planes(self):
        l = self.l
        for copy in self.zc:
            copy.wait_recv()

        def body(n, carry):
            by, bx = n // 2, n % 2
            add_into(
                self.block(l.z, by, bx), *[self.zb.at[k, by, bx] for k in range(l.zs - 1)]
            )
            return carry

        lax.fori_loop(0, 4, body, 0)
        peer3, peer2, (y3, x3), (y2, x2) = self.over
        self.c3 = self.send(0, lambda: self.block(l.z, 1 - l.y, 1 - l.x), lambda: self.diag, peer3)
        self.cn = self.send(1, lambda: self.block(l.z, y3, x3), lambda: self.n3, peer3)

    def add_diag(self):
        l = self.l
        peer3, peer2, (y3, x3), (y2, x2) = self.over
        self.c3.wait_recv()
        add_into(self.block(l.z, y2, x2), self.diag)
        self.c2 = self.send(2, lambda: self.block(l.z, y2, x2), lambda: self.n2, peer2)

    def total(self):
        l = self.l
        self.cn.wait_recv()
        self.c2.wait_recv()
        own = self.block(l.z, l.y, l.x)[...].astype(F32)
        return own + self.n3[...].astype(F32) + self.n2[...].astype(F32)


def dot(left, right):
    return jnp.dot(left, right, preferred_element_type=F32)


def dot_t(left, right):
    return lax.dot_general(left, right, (((1,), (1,)), ((), ())), preferred_element_type=F32)


def t_dot(left, right):
    return lax.dot_general(left, right, (((0,), (0,)), ((), ())), preferred_element_type=F32)


def lanes(shape):
    return lax.broadcasted_iota(jnp.int32, shape, len(shape) - 1)


def rows_of(shape):
    return lax.broadcasted_iota(jnp.int32, shape, len(shape) - 2)


def turn(part, cosine, sine, direction):
    swapped = jnp.where(
        lanes(part.shape) % HD < HD // 2,
        pltpu.roll(part, 128 - HD // 2, 1),
        pltpu.roll(part, HD // 2, 1),
    )
    return part * cosine + (direction * swapped) * sine


def rows_mean(values):
    return jnp.sum(values, axis=-1, keepdims=True) * (1.0 / values.shape[-1])


def selection(width, lane, start, columns):
    shape = (VECTOR_TILE[1], columns)
    column = (lanes(shape) + start).astype(F32)
    owner = jnp.floor((column + 0.5) * (1.0 / width))
    within = (column - owner * width).astype(jnp.int32) + lane
    return jnp.where(rows_of(shape) == within, 1.0, 0.0).astype(BF16)


def owner_mask(width, row, start, columns, devices):
    shape = (devices * VECTOR_TILE[0], columns)
    packed_row = rows_of(shape)
    first = (packed_row // VECTOR_TILE[0]) * width
    column = lanes(shape) + start
    return (
        (packed_row % VECTOR_TILE[0] == row) & (column >= first) & (column < first + width)
    )


def each_vector_tile(widths, tile, body, carry):
    devices = tile // widths[1]
    for i, row in ((JOINT_B, 0), (EXPAND_B, 1)):
        carry = lax.fori_loop(
            0,
            widths[i] * devices // tile,
            lambda n, inner, i=i, row=row: body(
                i, row, 0, widths[i], pl.multiple_of(n * tile, 128), inner
            ),
            carry,
        )
    return lax.fori_loop(
        0,
        6,
        lambda n, inner: body(
            n + 1 + n // 3, 2 + n // 3, (n % 3) * widths[1], widths[1], 0, inner
        ),
        carry,
    )


JOINT_B, OUTPUT_B, GAIN1, SHIFT1, EXPAND_B, REDUCE_B, GAIN2, SHIFT2 = range(8)


def layer_kernel(
    zs,
    widths,
    lens,
    freq,
    jw,
    ow,
    ew,
    rw,
    vec,
    tok,
    cot,
    y_out,
    gx_out,
    gj,
    go,
    ge,
    gr,
    gv,
    prob_hbm,
    J,
    O,
    E,
    R,
    V,
    T,
    stage_j,
    stage_o,
    stage_e,
    pair_j,
    pair_o,
    pair_e,
    cos_t,
    sin_t,
    Q,
    K,
    VV,
    ATT,
    X1,
    I1,
    HL,
    FX,
    DRED,
    COT,
    BIAS,
    GVEC,
    MASK,
    SR,
    SE,
    SO,
    SJ,
    SV,
    r1_bufs,
    r2_bufs,
    e_bufs,
    o_bufs,
    j_bufs,
    v_bufs,
    SX,
    RX,
    pair_sems,
    gather_sems,
    tok_sems,
    first_sems,
    scatter_sems,
    last_sems,
    far_sems,
    local_sems,
    prob_sems,
    VG,
):
    l = Links(zs)
    z, y, x, c = l.z, l.y, l.x, l.c
    micro, shard, width = Q.shape
    own_rows = micro * shard
    ff = zs * 8 * rw.shape[0]
    devices = zs * 8
    groups = width // 128
    pack = 4 * shard
    full = [w * devices for w in widths]

    cot_in = pltpu.make_async_copy(cot, COT, local_sems.at[0])
    cot_in.start()
    tok_in = pltpu.make_async_copy(tok, T.at[x, c], local_sems.at[1])
    tok_in.start()
    greet([l.sib, l.xpeer, l.ypeer] + l.zpeers)

    def halves(ref):
        return (
            lambda bz, by, bx: ref.at[c, bz, by, bx],
            lambda by, bx: ref.at[c, :, by, bx],
        )

    def natural(ref):
        return (
            lambda bz, by, bx: ref.at[bz, by, bx, c],
            lambda by, bx: ref.at[:, by, bx, c],
        )

    split = rw.shape[0] // 2
    low, high = pl.ds(0, split), pl.ds(split, split)
    gV = GatherZFirst(l, gather_sems, 0, *natural(V))
    gJ = GatherZFirst(l, gather_sems, 1, *halves(J))
    gO = GatherZFirst(l, gather_sems, 2, *halves(O))
    gE = GatherZFirst(l, gather_sems, 3, *halves(E))
    gR1 = GatherZFirst(
        l,
        gather_sems,
        4,
        lambda bz, by, bx: R.at[bz, by, bx, c, low],
        lambda by, bx: R.at[:, by, bx, c, low],
    )
    gR2 = GatherZLast(
        l,
        gather_sems,
        5,
        lambda bz, by, bx: R.at[bz, by, bx, c, high],
        lambda bz: R.at[bz, :, :, c, high],
    )
    pairs = []
    for i, (w, stage, pair) in enumerate(
        ((jw, stage_j, pair_j), (ow, stage_o, pair_o), (ew, stage_e, pair_e))
    ):
        half = stage.shape[2]
        stage[0] = w[:, :half].astype(F32)
        stage[1] = w[:, half:].astype(F32)
        copy = remote(stage.at[1 - c], pair, pair_sems, i, l.sib)
        copy.start()
        pairs.append(copy)
    R[z, y, x, c] = rw[...]
    V[z, y, x, c] = vec[...]
    gR2.start()
    tok_in.wait()
    tok_x = remote(T.at[x, c], T.at[x, c], tok_sems, 0, l.xpeer)
    tok_s = remote(T.at[x, c], T.at[x, c], tok_sems, 1, l.sib)
    tok_x.start()
    tok_s.start()
    gV.start()

    def pair_up(n, W, stage, pair):
        pairs[n].wait_recv()
        mine = stage[c]
        other = pair[...]
        first = jnp.where(c == 0, mine, other)
        second = jnp.where(c == 0, other, mine)
        W[c, z, y, x] = jnp.concatenate([first, second], axis=0).astype(BF16)

    pair_up(0, J, stage_j, pair_j)
    gJ.start()
    pair_up(1, O, stage_o, pair_o)
    gO.start()
    pair_up(2, E, stage_e, pair_e)
    gE.start()
    gR1.start()
    gR2.forward()

    def ends_of(m):
        ends, total = [], 0
        for j in range(lens.shape[1]):
            total = total + lens[m, j]
            ends.append(total)
        return ends

    def tables(n, carry):
        b, m = n // micro, n % micro
        position = b * shard + rows_of((shard, 128))
        begin = jnp.zeros((shard, 128), jnp.int32)
        for end in ends_of(m):
            begin = jnp.where(position >= end, end, begin)
        angle = (position - begin).astype(F32) * freq[0:1, :]
        cos_t[b, m] = jnp.cos(angle)
        sine = jnp.sin(angle)
        sin_t[b, m] = jnp.where(lanes((shard, 128)) % HD < HD // 2, -sine, sine)
        return carry

    lax.fori_loop(0, 4 * micro, tables, 0)
    GVEC[...] = jnp.zeros_like(GVEC)

    gV.columns()
    gJ.columns()
    gO.columns()
    gV.forward()
    gJ.forward()
    gE.columns()
    gO.forward()
    gV.last()
    tok_x.wait_recv()
    tok_f = remote(T.at[1 - x, c], T.at[1 - x, c], tok_sems, 2, l.sib)
    tok_f.start()
    gJ.last()
    gR1.columns()
    gR2.planes()

    gV.finish()
    def unpack(i, row, lane, w, start, carry):
        packed = V[...].reshape(devices * VECTOR_TILE[0], VECTOR_TILE[1]).astype(BF16)
        spread = dot(packed, selection(w, lane, start, width))
        mine = jnp.where(owner_mask(w, row, start, width, devices), spread, 0.0)
        BIAS[pl.ds(i, 1), pl.ds(start, width)] = jnp.sum(mine, axis=0, keepdims=True)
        return carry

    each_vector_tile(widths, width, unpack, 0)

    def bias(i, start=0, size=None):
        size = full[i] if size is None else size
        return BIAS[i : i + 1, pl.ds(start, size)]

    kc = J.shape[5] - width

    def flat(ref, *index):
        value = ref[index]
        return value.reshape((-1, value.shape[-1]))

    def wide(ref, h, start, size):
        return ref[h, :, :, :, :, pl.ds(start, size)].reshape(-1, size)

    def rotated(values, cosine, sine, direction):
        parts = []
        for g in range(values.shape[1] // 128):
            parts.append(turn(values[:, g * 128 : (g + 1) * 128], cosine, sine, direction))
        return jnp.concatenate(parts, axis=1)

    gJ.finish()
    joint_q = dot(flat(T, x, c), wide(J, 0, 0, width)) + bias(JOINT_B, 0, width)
    own_blk = x * 2 + c
    Q[...] = (
        (rotated(joint_q, flat(cos_t, own_blk), flat(sin_t, own_blk), 1.0).astype(BF16))
        * jnp.asarray(HD ** (-0.5), BF16)
    ).reshape(Q.shape)
    gE.forward()
    tok_s.wait_recv()
    tok_f.wait_recv()

    def project(b, carry):
        tokens_b = flat(T, b // 2, b % 2)
        cosine, sine = flat(cos_t, b), flat(sin_t, b)
        k0 = dot(tokens_b, wide(J, 0, width, kc)) + bias(JOINT_B, width, kc)
        K[b, :, :, :kc] = (
            rotated(k0, cosine, sine, 1.0).astype(BF16).reshape(micro, shard, kc)
        )
        k1 = dot(tokens_b, wide(J, 1, 0, width - kc)) + bias(JOINT_B, width + kc, width - kc)
        K[b, :, :, kc:] = (
            rotated(k1, cosine, sine, 1.0).astype(BF16).reshape(micro, shard, width - kc)
        )
        v = dot(tokens_b, wide(J, 1, width - kc, width)) + bias(JOINT_B, 2 * width, width)
        VV[b] = v.astype(BF16).reshape(micro, shard, width)
        return carry

    lax.fori_loop(0, 4, project, 0)
    gR1.forward()
    gO.last()

    oh = O.shape[5]

    first_head = lanes((shard, 128)) < HD

    def stacked(part):
        zero = jnp.zeros_like(part)
        return jnp.concatenate(
            [jnp.where(first_head, part, zero), jnp.where(first_head, zero, part)], axis=0
        )

    def unstacked(part):
        return jnp.where(first_head, part[:shard], part[shard:])

    def attention(PR):
        def attend(m, carry):
            ends = ends_of(m)
            query_at = own_blk * shard + rows_of((shard, pack))
            key_at = lanes((shard, pack))
            query_seg = jnp.zeros((shard, pack), jnp.int32)
            key_seg = jnp.zeros((shard, pack), jnp.int32)
            for end in ends:
                query_seg = query_seg + (query_at >= end).astype(jnp.int32)
                key_seg = key_seg + (key_at >= end).astype(jnp.int32)
            MASK[...] = jnp.where(query_seg == key_seg, 0.0, NEGATIVE)

            def group(j, inner):
                at = pl.ds(pl.multiple_of(j * 128, 128), 128)
                q = stacked(Q[m, :, at])
                k = K[:, m, :, at].reshape(pack, 128)
                v = VV[:, m, :, at].reshape(pack, 128)
                scores = dot_t(q, k)
                mask = MASK[...]
                scores = scores + jnp.concatenate([mask, mask], axis=0)
                weights = jnp.exp(scores - jnp.max(scores, axis=-1, keepdims=True))
                prob = weights * (1.0 / jnp.sum(weights, axis=-1, keepdims=True))
                prob = prob.astype(BF16)
                PR[m, j] = prob
                ATT[m, :, at] = unstacked(dot(prob, v)).astype(BF16)
                return inner

            lax.fori_loop(0, groups, group, 0)
            pltpu.make_async_copy(PR.at[m], prob_hbm.at[m], prob_sems.at[m]).start()
            return carry

        lax.fori_loop(0, micro, attend, 0)
        gO.finish()
        gE.last()

        attended = ATT[...].reshape(own_rows, width)
        FX[:, :, :oh] = dot(attended, wide(O, 0, 0, oh)).reshape(micro, shard, oh)
        FX[:, :, oh:] = dot(attended, wide(O, 1, 0, oh)).reshape(micro, shard, oh)

        def first_norm(m, carry):
            residual = T[x, c, m].astype(F32) + (FX[m] + bias(OUTPUT_B))
            centered = residual - rows_mean(residual)
            inverse = lax.rsqrt(rows_mean(centered * centered) + EPSILON)
            normal = centered * inverse
            X1[m] = normal
            I1[m] = jnp.broadcast_to(inverse, (shard, 128))
            HL[m] = (normal * bias(GAIN1) + bias(SHIFT1)).astype(BF16)
            return carry

        lax.fori_loop(0, micro, first_norm, 0)
        for m in range(micro):
            pltpu.make_async_copy(PR.at[m], prob_hbm.at[m], prob_sems.at[m]).wait()

    prob_shape = pltpu.VMEM((micro, groups, 2 * shard, pack), BF16)
    pl.run_scoped(attention, prob_shape)
    gR1.last()
    gE.finish()
    tile = ff // zs
    per_half = zs // 2
    hidden_low = lambda: HL[...].reshape(own_rows, width)

    def feed_forward(ACT, GP):
        def expand(n, carry):
            h, t = n // per_half, n % per_half
            to = pl.ds(pl.multiple_of(n * tile, 128), tile)
            weight = E[h, :, :, :, :, pl.ds(pl.multiple_of(t * tile, 128), tile)]
            value = dot(hidden_low(), weight.reshape(width, tile)) + BIAS[
                EXPAND_B : EXPAND_B + 1, to
            ]
            scale = math.sqrt(2.0 / math.pi)
            square = value * value
            t_value = jnp.tanh(value * (scale + (scale * 0.044715) * square))
            half = 0.5 * (1.0 + t_value)
            ACT[:, :, to] = (value * half).astype(BF16).reshape(micro, shard, tile)
            slope = half + value * (0.5 * (1.0 - t_value * t_value)) * (
                scale + (3.0 * scale * 0.044715) * square
            )
            GP[:, :, to] = slope.astype(BF16).reshape(micro, shard, tile)
            return carry

        lax.fori_loop(0, zs, expand, 0)
        gR2.last()
        gR1.finish()
        gR2.finish()
        cot_in.wait()

        chunk = 2

        def reduce(n, carry):
            at = pl.ds(n * chunk, chunk)
            reduced = dot(
                ACT[at].reshape(chunk * shard, ff), R[...].reshape(ff, width)
            ) + bias(REDUCE_B)
            hidden = X1[at].reshape(chunk * shard, width) * bias(GAIN1) + bias(SHIFT1)
            residual = hidden + reduced
            centered = residual - rows_mean(residual)
            inverse = lax.rsqrt(rows_mean(centered * centered) + EPSILON)
            normal = centered * inverse
            HLY = (normal * bias(GAIN2) + bias(SHIFT2)).astype(BF16)
            DY = COT[at].reshape(chunk * shard, width).astype(F32)
            COT[at] = HLY.reshape(chunk, shard, width)
            GVEC[GAIN2 : GAIN2 + 1, :width] += jnp.sum(DY * normal, axis=0, keepdims=True)
            GVEC[SHIFT2 : SHIFT2 + 1, :width] += jnp.sum(DY, axis=0, keepdims=True)
            dn = DY * bias(GAIN2)
            grad = inverse * (dn - rows_mean(dn) - normal * rows_mean(dn * normal))
            FX[at] = grad.reshape(chunk, shard, width)
            grad_low = grad.astype(BF16)
            DRED[at] = grad_low.reshape(chunk, shard, width)
            GVEC[REDUCE_B : REDUCE_B + 1, :width] += jnp.sum(
                grad_low.astype(F32), axis=0, keepdims=True
            )
            return carry

        lax.fori_loop(0, micro // chunk, reduce, 0)
        pltpu.make_async_copy(COT, y_out, local_sems.at[2]).start()
        for item in (gV, gJ, gO, gE, gR1, gR2):
            item.drain()
        for copy in pairs + [tok_x, tok_s, tok_f]:
            copy.wait_send()

        def back_reduce(n, carry):
            at = pl.ds(pl.multiple_of(n * tile, 128), tile)
            dred = DRED[...].reshape(own_rows, width)
            grad = dot_t(dred, flat(R, n))
            grad = grad * GP[:, :, at].reshape(own_rows, tile).astype(F32)
            grad_low = grad.astype(BF16)
            GP[:, :, at] = grad_low.reshape(micro, shard, tile)
            GVEC[EXPAND_B : EXPAND_B + 1, at] = jnp.sum(
                grad_low.astype(F32), axis=0, keepdims=True
            )
            weight_grad = t_dot(ACT[:, :, at].reshape(own_rows, tile), dred)
            R[n] = weight_grad.astype(BF16).reshape(R.shape[1:])
            remote(R.at[n, :, :, 1 - c], SR.at[n], first_sems, (0, n), l.sib).start()
            return carry

        lax.fori_loop(0, zs, back_reduce, 0)
        for h in range(2):
            part = pl.ds(h * (ff // 2), ff // 2)
            FX[...] += dot_t(
                GP[:, :, part].reshape(own_rows, ff // 2), wide(E, h, 0, ff // 2)
            ).reshape(micro, shard, width)
        for turn_at in range(2):
            h = pick(c, 1 - turn_at, turn_at)

            def back_expand(t, carry, h=h):
                at = pl.ds(pl.multiple_of((h * per_half + t) * tile, 128), tile)
                grad = t_dot(hidden_low(), GP[:, :, at].reshape(own_rows, tile))
                E[h, :, :, :, :, pl.ds(pl.multiple_of(t * tile, 128), tile)] = grad.astype(
                    BF16
                ).reshape(zs, 2, 2, E.shape[4], tile)
                return carry

            lax.fori_loop(0, per_half, back_expand, 0)
            if turn_at == 0:
                remote(E.at[1 - c], SE, first_sems, (1, 0), l.sib).start()

    pl.run_scoped(
        feed_forward,
        pltpu.VMEM((micro, shard, ff), BF16),
        pltpu.VMEM((micro, shard, ff), BF16),
    )

    firstE = [Again(lambda: remote(E.at[1 - c], SE, first_sems, (1, 0), l.sib))]

    def sums(ref):
        return (lambda bz, by, bx: ref.at[bz, by, bx]), (lambda by, bx: ref.at[:, by, bx])

    def own_half(ref):
        return lambda bz, by, bx: ref.at[c, bz, by, bx]

    sR1 = ScatterZFirst(
        l,
        scatter_sems,
        0,
        (
            lambda bz, by, bx: SR.at[bz, by, bx, low],
            lambda by, bx: SR.at[:, by, bx, low],
        ),
        r1_bufs,
        lambda bz, by, bx: R.at[bz, by, bx, c, low],
        l.over_y,
    )
    sR2 = ScatterZLast(
        l,
        scatter_sems,
        1,
        (lambda bz, by, bx: SR.at[bz, by, bx, high], lambda bz: SR.at[bz, :, :, high]),
        r2_bufs,
        lambda bz, by, bx: R.at[bz, by, bx, c, high],
        l.mix,
    )
    sE = ScatterZFirst(l, scatter_sems, 2, sums(SE), e_bufs, own_half(E), l.mix)
    sO = ScatterZFirst(l, scatter_sems, 3, sums(SO), o_bufs, own_half(O), l.over_y)
    sV = ScatterZFirst(
        l, scatter_sems, 5, sums(SV), v_bufs, lambda bz, by, bx: VG.at[bz, by, bx, c], l.mix
    )
    firstR = [
        Again(lambda n=n: remote(R.at[n, :, :, 1 - c], SR.at[n], first_sems, (0, n), l.sib))
        for n in range(zs)
    ]
    sR1.add_sib(firstR)
    sR2.add_sib([])

    firstO = Again(lambda: remote(O.at[1 - c], SO, first_sems, (2, 0), l.sib))

    def back_attention(PR):
        def fetch(m):
            return pltpu.make_async_copy(prob_hbm.at[m], PR.at[m], prob_sems.at[m])

        for m in range(micro):
            fetch(m).start()

        def back_norm(m, carry):
            grad = FX[m]
            normal = X1[m]
            GVEC[GAIN1 : GAIN1 + 1, :width] += jnp.sum(grad * normal, axis=0, keepdims=True)
            GVEC[SHIFT1 : SHIFT1 + 1, :width] += jnp.sum(grad, axis=0, keepdims=True)
            dn = grad * bias(GAIN1)
            grad = I1[m][:, :1] * (dn - rows_mean(dn) - normal * rows_mean(dn * normal))
            FX[m] = grad
            grad_low = grad.astype(BF16)
            DRED[m] = grad_low
            GVEC[OUTPUT_B : OUTPUT_B + 1, :width] += jnp.sum(
                grad_low.astype(F32), axis=0, keepdims=True
            )
            return carry

        lax.fori_loop(0, micro, back_norm, 0)
        sE.add_sib(firstE)
        branch_grad = lambda: DRED[...].reshape(own_rows, width)
        attended_grad = dot_t(branch_grad()[:, :oh], wide(O, 0, 0, oh)) + dot_t(
            branch_grad()[:, oh:], wide(O, 1, 0, oh)
        )
        HL[...] = attended_grad.astype(BF16).reshape(HL.shape)
        for h in range(2):
            grad = t_dot(ATT[...].reshape(own_rows, width), branch_grad()[:, h * oh : (h + 1) * oh])
            O[h] = grad.astype(BF16).reshape(O.shape[1:])
        firstO.start()
        sR1.add_diag()
        sR2.add_planes()
        sO.add_sib([firstO])
        sE.add_diag()

        def back_attend(m, carry):
            fetch(m).wait()

            def group(j, inner):
                start = pl.multiple_of(j * 128, 128)
                at = pl.ds(start, 128)
                prob = PR[m, j]
                d_out = stacked(HL[m, :, at])
                k = K[:, m, :, at].reshape(pack, 128)
                v = VV[:, m, :, at].reshape(pack, 128)
                q = stacked(Q[m, :, at])
                prob_grad = dot_t(d_out, v)
                prob_float = prob.astype(F32)
                product = prob_float * prob_grad
                delta = jnp.sum(product, axis=-1, keepdims=True)
                score_grad = (product - prob_float * delta).astype(BF16)
                dq = unstacked(dot(score_grad, k)) * (HD ** (-0.5))
                dk = t_dot(score_grad, q)
                dv = t_dot(prob, d_out).astype(BF16)
                dq = turn(dq, cos_t[own_blk, m], sin_t[own_blk, m], -1.0).astype(BF16)
                dk = turn(
                    dk,
                    cos_t[:, m].reshape(pack, 128),
                    sin_t[:, m].reshape(pack, 128),
                    -1.0,
                ).astype(BF16)
                DRED[m, :, at] = dq
                K[:, m, :, at] = dk.reshape(4, shard, 128)
                VV[:, m, :, at] = dv.reshape(4, shard, 128)
                for n, part in enumerate((dq, dk, dv)):
                    to = pl.ds(pl.multiple_of(start + n * width, 128), 128)
                    GVEC[JOINT_B : JOINT_B + 1, to] += jnp.sum(
                        part.astype(F32), axis=0, keepdims=True
                    )
                return inner

            lax.fori_loop(0, groups, group, 0)
            return carry

        lax.fori_loop(0, micro, back_attend, 0)
    pl.run_scoped(back_attention, prob_shape)
    sR1.add_near()
    sR2.add_diag()

    VG[...] = jnp.zeros_like(VG)

    def pack_grads(i, row, lane, w, start, carry):
        line = GVEC[pl.ds(i, 1), pl.ds(start, width)]
        high_part = line.astype(BF16).astype(F32)
        low_part = line - high_part
        keep = owner_mask(w, row, start, width, devices)
        chosen = selection(w, lane, start, width)
        grads = dot_t(jnp.where(keep, high_part, 0.0).astype(BF16), chosen)
        grads = grads + dot_t(jnp.where(keep, low_part, 0.0).astype(BF16), chosen)
        VG[...] += grads.reshape(VG.shape)
        return carry

    each_vector_tile(widths, width, pack_grads, 0)
    firstV = remote(VG.at[:, :, :, 1 - c], SV, first_sems, (4, 0), l.sib)
    firstV.start()

    def joint(GJ):
        feats = width // 2

        def joint_rows(n, carry):
            at = pl.ds(pl.multiple_of(n * feats, 128), feats)
            to = pl.ds(n * (zs // 2), zs // 2)

            def put(h, start, grad):
                GJ[h, to, :, :, :, pl.ds(start, grad.shape[1])] = grad.astype(BF16).reshape(
                    zs // 2, 2, 2, GJ.shape[4], grad.shape[1]
                )

            tokens_own = T[x, c, :, :, at].reshape(own_rows, feats)
            put(0, 0, t_dot(tokens_own, DRED[...].reshape(own_rows, width)))
            tokens_all = lambda: T[:, :, :, :, at].reshape(4 * own_rows, feats)
            keys = lambda s, n: K[:, :, :, pl.ds(s, n)].reshape(4 * own_rows, n)
            put(0, width, t_dot(tokens_all(), keys(0, kc)))
            put(1, 0, t_dot(tokens_all(), keys(kc, width - kc)))
            put(1, width - kc, t_dot(tokens_all(), VV[...].reshape(4 * own_rows, width)))
            return carry

        lax.fori_loop(0, 2, joint_rows, 0)
        firstJ = remote(GJ.at[1 - c], SJ, first_sems, (3, 0), l.sib)
        firstJ.start()
        sJ = ScatterZFirst(l, scatter_sems, 4, sums(SJ), j_bufs, own_half(GJ), l.over_y)
        sE.add_near()
        sO.add_diag()

        FX[...] += dot_t(
            DRED[...].reshape(own_rows, width), wide(J, 0, 0, width)
        ).reshape(FX.shape)
        sJ.add_sib([firstJ])
        sV.add_sib([firstV])

        def far(b, carry):
            keys_b = flat(K, b)
            grad = dot_t(keys_b[:, :kc], wide(J, 0, width, kc))
            grad = grad + dot_t(keys_b[:, kc:], wide(J, 1, 0, width - kc))
            grad = grad + dot_t(flat(VV, b), wide(J, 1, width - kc, width))
            T[b // 2, b % 2] = grad.astype(BF16).reshape(T.shape[2:])
            return carry

        lax.fori_loop(0, 4, far, 0)
        far_sib = remote(T.at[:, 1 - c], SX, far_sems, 0, l.sib)
        far_sib.start()
        sJ.add_diag()
        sV.add_diag()
        sO.add_near()
        far_sib.wait_recv()
        for n in range(2):
            add_into(SX.at[n], T.at[n, c])
        far_x = remote(SX.at[1 - x], RX, far_sems, 1, l.xpeer)
        far_x.start()

        def settle(item, n, out, stage, pair):
            total = item.total()
            stage[0] = total[: stage.shape[1]]
            stage[1] = total[stage.shape[1] :]
            copy = remote(stage.at[1 - c], pair, last_sems, n, l.sib)
            copy.start()
            return copy

        def place_halves(copy, out, stage, pair):
            copy.wait_recv()
            half = stage.shape[2]
            mine = stage[c]
            other = pair[...]
            out[:, :half] = jnp.where(c == 0, mine, other)
            out[:, half:] = jnp.where(c == 0, other, mine)

        gr[:split] = sR1.total()
        gr[split:] = sR2.total()
        lastE = settle(sE, 0, ge, stage_e, pair_e)
        lastO = settle(sO, 1, go, stage_o, pair_o)
        place_halves(lastE, ge, stage_e, pair_e)
        place_halves(lastO, go, stage_o, pair_o)
        sJ.add_near()
        sV.add_near()
        far_x.wait_recv()

        def last_x(m, carry):
            FX[m] = FX[m] + SX[x, m].astype(F32) + RX[m].astype(F32)
            return carry

        lax.fori_loop(0, micro, last_x, 0)
        x_copy = pltpu.make_async_copy(FX, gx_out, local_sems.at[3])
        x_copy.start()
        lastJ = settle(sJ, 2, gj, stage_j, pair_j)
        gv[...] = sV.total()
        place_halves(lastJ, gj, stage_j, pair_j)
        x_copy.wait()
        pltpu.make_async_copy(COT, y_out, local_sems.at[2]).wait()
        for copy in firstR + firstE + [firstO, firstJ, firstV, far_sib, far_x]:
            copy.wait_send()
        for copy in (lastE, lastO, lastJ):
            copy.wait_send()
        for item in (sR1, sR2, sE, sO, sJ, sV):
            item.drain()

    pl.run_scoped(joint, pltpu.VMEM(J.shape, BF16))


def layer(zs, widths, lengths, weights, vec, tok, cot):
    jw, ow, ew, rw = weights
    micro, shard, width = tok.shape
    vmem = pl.BlockSpec(memory_space=pltpu.VMEM)
    hbm = pl.BlockSpec(memory_space=pl.ANY)
    smem = pl.BlockSpec(memory_space=pltpu.SMEM)
    devices = zs * 8
    pack = 4 * shard
    ff = devices * rw.shape[0]
    paired = (jw, ow, ew)
    dma = pltpu.SemaphoreType.DMA

    def sems(*shape):
        return (dma(shape), dma(shape))

    def halves(w):
        return (2, zs, 2, 2, 2 * w.shape[0], w.shape[1] // 2)

    def reduction(shape, dtype=BF16):
        column = (zs,) + shape
        return (
            pltpu.VMEM(column, dtype),
            pltpu.VMEM(column, dtype),
            pltpu.VMEM(column, dtype),
            pltpu.VMEM((zs - 1,) + shape, dtype),
        )

    r2_block = (rw.shape[0] // 2, rw.shape[1])
    r2_bufs = (
        pltpu.VMEM(r2_block, BF16),
        pltpu.VMEM(r2_block, BF16),
        pltpu.VMEM(r2_block, BF16),
        pltpu.VMEM((zs - 1, 2, 2) + r2_block, BF16),
    )
    rows = (micro, shard, width)
    scratch = (
        [pltpu.VMEM(halves(w), BF16) for w in paired]
        + [
            pltpu.VMEM((zs, 2, 2, 2) + rw.shape, BF16),
            pltpu.VMEM((zs, 2, 2, 2) + VECTOR_TILE, F32),
            pltpu.VMEM((2, 2) + rows, BF16),
        ]
        + [pltpu.VMEM((2, w.shape[0], w.shape[1] // 2), F32) for w in paired]
        + [pltpu.VMEM((w.shape[0], w.shape[1] // 2), F32) for w in paired]
        + [
            pltpu.VMEM((4, micro, shard, 128), F32),
            pltpu.VMEM((4, micro, shard, 128), F32),
            pltpu.VMEM(rows, BF16),
            pltpu.VMEM((4,) + rows, BF16),
            pltpu.VMEM((4,) + rows, BF16),
            pltpu.VMEM(rows, BF16),
            pltpu.VMEM(rows, F32),
            pltpu.VMEM((micro, shard, 128), F32),
            pltpu.VMEM(rows, BF16),
            pltpu.VMEM(rows, F32),
            pltpu.VMEM(rows, BF16),
            pltpu.VMEM(rows, BF16),
            pltpu.VMEM((8, ff), F32),
            pltpu.VMEM((8, ff), F32),
            pltpu.VMEM((shard, pack), F32),
            pltpu.VMEM((zs, 2, 2) + rw.shape, BF16),
        ]
        + [pltpu.VMEM(halves(w)[1:], BF16) for w in (ew, ow, jw)]
        + [
            pltpu.VMEM((zs, 2, 2) + VECTOR_TILE, F32),
            reduction(r2_block),
            r2_bufs,
        ]
        + [reduction(halves(w)[4:]) for w in (ew, ow, jw)]
        + [
            reduction(VECTOR_TILE, F32),
            pltpu.VMEM((2,) + rows, BF16),
            pltpu.VMEM(rows, BF16),
            sems(3),
            sems(6, zs + 6),
            sems(3),
            sems(5, zs),
            sems(6, zs + 2),
            sems(3),
            sems(2),
            dma((4,)),
            dma((micro,)),
            pltpu.VMEM((zs, 2, 2, 2) + VECTOR_TILE, F32),
        ]
    )
    frequency = 10000.0 ** (-(np.arange(128) % (HD // 2)) * (2.0 / HD))
    freq = jnp.asarray(np.broadcast_to(frequency.astype(np.float32), (8, 128)))
    shapes = [
        jax.ShapeDtypeStruct(rows, BF16),
        jax.ShapeDtypeStruct(rows, F32),
        jax.ShapeDtypeStruct(jw.shape, F32),
        jax.ShapeDtypeStruct(ow.shape, F32),
        jax.ShapeDtypeStruct(ew.shape, F32),
        jax.ShapeDtypeStruct(rw.shape, F32),
        jax.ShapeDtypeStruct(VECTOR_TILE, F32),
        jax.ShapeDtypeStruct((micro, width // 128, 2 * shard, pack), BF16),
    ]
    return pl.pallas_call(
        functools.partial(layer_kernel, zs, widths),
        out_shape=shapes,
        in_specs=[smem] + [vmem] * 6 + [hbm] * 2,
        out_specs=[hbm] * 2 + [vmem] * 5 + [hbm],
        scratch_shapes=scratch,
        compiler_params=pltpu.CompilerParams(
            collective_id=0, has_side_effects=True, vmem_limit_bytes=64 << 20
        ),
    )(lengths, freq, jw, ow, ew, rw, vec, tok, cot)[:-1]


def layout(lengths, places):
    doc_ends = jnp.cumsum(lengths)
    starts = doc_ends - lengths
    segment = jnp.sum((places[:, None] >= doc_ends[None, :]).astype(jnp.int32), axis=1)
    labels = jnp.arange(lengths.shape[0], dtype=jnp.int32)
    doc_begin = jnp.sum(jnp.where(segment[:, None] == labels[None, :], starts[None, :], 0), axis=1)
    doc_begin = jnp.where(segment == lengths.shape[0], doc_ends[-1], doc_begin)
    return (segment, places - doc_begin)


def rotate(entries, angles, direction):
    half_width = HD // 2
    cosine = jnp.cos(angles)[:, :, None, :]
    sine_part = direction * jnp.sin(angles)[:, :, None, :]
    pieces = entries.reshape(entries.shape[0], entries.shape[1], -1, HD)
    first_half = pieces[..., :half_width]
    second_half = pieces[..., half_width:]
    turned = jnp.concatenate(
        [
            first_half * cosine - second_half * sine_part,
            second_half * cosine + first_half * sine_part,
        ],
        axis=-1,
    )
    return turned.reshape(entries.shape)


def normalize(residual, gain_vector, offset):
    centered = residual - jnp.mean(residual, axis=-1, keepdims=True)
    inverse_std = lax.rsqrt(jnp.mean(centered * centered, axis=-1, keepdims=True) + EPSILON)
    return centered * inverse_std * gain_vector + offset


def contract_rows(left, right):
    return lax.dot_general(
        left, right, (((0,), (0,)), ((), ())), preferred_element_type=F32
    )


def times_transposed(left, right):
    return lax.dot_general(
        left, right, (((1,), (1,)), ((), ())), preferred_element_type=F32
    )


def column_sum(values):
    return jnp.sum(values.astype(F32), axis=0)


def per_device(
    mesh_shape,
    tokens,
    document_lengths,
    joint_weight,
    joint_bias,
    output_weight,
    output_bias,
    first_gain,
    first_shift,
    expand_weight,
    expand_bias,
    reduce_weight,
    reduce_bias,
    second_gain,
    second_shift,
    cotangent,
):
    dp_size, blk_size = mesh_shape
    micro, _, shard_rows, width = tokens.shape
    own = micro * shard_rows
    pack_rows = shard_rows * blk_size
    vectors = (
        joint_bias,
        output_bias,
        first_gain,
        first_shift,
        expand_bias,
        reduce_bias,
        second_gain,
        second_shift,
    )
    widths = [v.shape[0] for v in vectors]
    use_kernels = (
        blk_size == 4 and dp_size % 2 == 0 and (2 * joint_weight.shape[0]) % 16 == 0
    )
    zs = dp_size // 2
    axes = ("dp", "blk")
    tokens_own = tokens[:, 0]
    if use_kernels:
        y, gx, gj, go, ge, gr, gv = layer(
            zs,
            widths,
            document_lengths[:, 0],
            (joint_weight, output_weight, expand_weight, reduce_weight),
            pack_vectors(vectors),
            tokens_own,
            cotangent[:, 0],
        )
        shares = unpack_vectors(gv, widths)
        return (y[:, None], gx[:, None], gj, shares[0], go) + tuple(shares[1:4]) + (
            ge,
            shares[4],
            gr,
        ) + tuple(shares[5:])
    joint_full, output_full, expand_full, reduce_full = (
        lax.all_gather(w, axes, axis=0, tiled=True)
        for w in (joint_weight, output_weight, expand_weight, reduce_weight)
    )
    packed = lax.all_gather(jnp.concatenate(vectors), axes, axis=0)
    cuts = [sum(widths[: i + 1]) for i in range(len(widths) - 1)]
    vector_full = [
        v.reshape(-1).astype(F32) for v in jnp.split(packed, cuts, axis=1)
    ]
    pack = lax.all_gather(tokens_own, "blk", axis=0)
    joint_b, output_b, gain1, shift1, expand_b, reduce_b, gain2, shift2 = vector_full

    pack_tokens = pack.transpose(1, 0, 2, 3).reshape(micro, pack_rows, width)
    lengths = document_lengths[:, 0]
    all_places = jnp.arange(pack_rows, dtype=jnp.int32)
    own_start = lax.axis_index("blk") * shard_rows
    key_segment, key_inner = jax.vmap(layout, (0, None))(lengths, all_places)
    segment = lax.dynamic_slice_in_dim(key_segment, own_start, shard_rows, 1)
    inner = lax.dynamic_slice_in_dim(key_inner, own_start, shard_rows, 1)
    frequency = 10000.0 ** (-jnp.arange(HD // 2, dtype=F32) * (2.0 / HD))
    key_angles = key_inner.astype(F32)[..., None] * frequency
    query_angles = inner.astype(F32)[..., None] * frequency
    score_scale = HD ** (-0.5)

    token_low = tokens_own.reshape(own, width)
    token_float = token_low.astype(F32)
    query_weight, pair_weight = joint_full[:, :width], joint_full[:, width:]
    query = jnp.dot(token_low, query_weight, preferred_element_type=F32) + joint_b[:width]
    query = rotate(query.reshape(micro, shard_rows, width), query_angles, 1.0).astype(BF16)
    pair = (
        jnp.dot(
            pack_tokens.reshape(micro * pack_rows, width),
            pair_weight,
            preferred_element_type=F32,
        )
        + joint_b[width:]
    ).reshape(micro, pack_rows, 2 * width)
    keys = rotate(pair[..., :width], key_angles, 1.0).astype(BF16)
    values = pair[..., width:].astype(BF16)
    query_heads = query.reshape(micro, shard_rows, H, HD)
    key_heads = keys.reshape(micro, pack_rows, H, HD)
    value_heads = values.reshape(micro, pack_rows, H, HD)
    allowed = (segment[:, :, None] == key_segment[:, None, :])[:, None]
    scores = (
        jnp.einsum("mqhd,mkhd->mhqk", query_heads, key_heads, preferred_element_type=F32)
        * score_scale
    )
    scores = jnp.where(allowed, scores, NEGATIVE)
    highest = jnp.max(scores, axis=-1, keepdims=True)
    weights = jnp.where(allowed, jnp.exp(scores - highest), 0.0)
    probability = weights / jnp.sum(weights, axis=-1, keepdims=True)
    probability_low = probability.astype(BF16)
    attended = (
        jnp.einsum("mhqk,mkhd->mqhd", probability_low, value_heads, preferred_element_type=F32)
        .reshape(own, width)
        .astype(BF16)
    )
    branch = jnp.dot(attended, output_full, preferred_element_type=F32) + output_b
    hidden, first_pullback = jax.vjp(normalize, token_float + branch, gain1, shift1)
    hidden_low = hidden.astype(BF16)
    expanded = jnp.dot(hidden_low, expand_full, preferred_element_type=F32) + expand_b
    active_float, gelu_pullback = jax.vjp(jax.nn.gelu, expanded)
    active = active_float.astype(BF16)
    reduced = jnp.dot(active, reduce_full, preferred_element_type=F32) + reduce_b
    result, second_pullback = jax.vjp(normalize, hidden + reduced, gain2, shift2)
    layer_output = result.astype(BF16).reshape(tokens.shape)

    second_residual, second_gain_grad, second_shift_grad = second_pullback(
        cotangent[:, 0].reshape(own, width).astype(F32)
    )
    reduced_grad = second_residual.astype(BF16)
    reduce_weight_grad = contract_rows(active, reduced_grad)
    reduce_bias_grad = column_sum(reduced_grad)
    (expanded_float,) = gelu_pullback(times_transposed(reduced_grad, reduce_full))
    expanded_grad = expanded_float.astype(BF16)
    expand_bias_grad = column_sum(expanded_grad)
    hidden_grad = second_residual + times_transposed(expanded_grad, expand_full)
    first_residual, first_gain_grad, first_shift_grad = first_pullback(hidden_grad)
    branch_grad = first_residual.astype(BF16)
    output_bias_grad = column_sum(branch_grad)
    attended_grad = times_transposed(branch_grad, output_full).astype(BF16)
    attended_heads = attended_grad.reshape(micro, shard_rows, H, HD)
    prob_grad = jnp.einsum(
        "mqhd,mkhd->mhqk", attended_heads, value_heads, preferred_element_type=F32
    )
    delta = jnp.sum(probability * prob_grad, axis=-1, keepdims=True)
    score_grad = (probability * (prob_grad - delta)).astype(BF16)
    query_grad = (
        jnp.einsum("mhqk,mkhd->mqhd", score_grad, key_heads, preferred_element_type=F32)
        * score_scale
    ).reshape(micro, shard_rows, width)
    key_grad = (
        jnp.einsum("mhqk,mqhd->mkhd", score_grad, query_heads, preferred_element_type=F32)
        * score_scale
    ).reshape(micro, pack_rows, width)
    value_grad = jnp.einsum(
        "mhqk,mqhd->mkhd", probability_low, attended_heads, preferred_element_type=F32
    ).reshape(micro, pack_rows, width)
    query_back = rotate(query_grad, query_angles, -1.0).reshape(own, width).astype(BF16)
    key_back = rotate(key_grad, key_angles, -1.0)
    pair_back = (
        jnp.concatenate([key_back, value_grad], axis=-1)
        .astype(BF16)
        .reshape(micro * pack_rows, 2 * width)
    )
    joint_bias_grad = jnp.concatenate([column_sum(query_back), column_sum(pair_back)])
    pack_flat = pack_tokens.reshape(micro * pack_rows, width)
    near_gradient = first_residual + times_transposed(query_back, query_weight)
    far_gradient = (
        times_transposed(pair_back, pair_weight)
        .astype(BF16)
        .reshape(micro, blk_size, shard_rows, width)
        .transpose(1, 0, 2, 3)
    )
    near_gradient = near_gradient.reshape(tokens_own.shape)
    vector_grads = (
        joint_bias_grad,
        output_bias_grad,
        first_gain_grad,
        first_shift_grad,
        expand_bias_grad,
        reduce_bias_grad,
        second_gain_grad,
        second_shift_grad,
    )
    joint_grad = jnp.concatenate(
        [contract_rows(token_low, query_back), contract_rows(pack_flat, pair_back)], axis=1
    )
    output_grad = contract_rows(attended, branch_grad)
    expand_grad = contract_rows(hidden_low, expanded_grad)
    gj, go, ge, gr = (
        lax.psum_scatter(g, axes, scatter_dimension=0, tiled=True)
        for g in (joint_grad, output_grad, expand_grad, reduce_weight_grad)
    )
    devices = dp_size * blk_size
    packed = jnp.concatenate([v.reshape(devices, -1) for v in vector_grads], axis=1)
    summed = lax.psum_scatter(packed, axes, scatter_dimension=0, tiled=True)
    cuts = [sum(widths[: i + 1]) for i in range(len(widths) - 1)]
    shares = [v.reshape(-1) for v in jnp.split(summed, cuts, axis=1)]
    far = lax.psum_scatter(far_gradient, "blk", scatter_dimension=0, tiled=True)
    input_gradient = near_gradient + far[0].astype(F32)
    return (
        layer_output,
        input_gradient[:, None],
        gj,
        shares[0],
        go,
        shares[1],
        shares[2],
        shares[3],
        ge,
        shares[4],
        gr,
        shares[5],
        shares[6],
        shares[7],
    )


def solution(mesh):
    rows = P(("dp", "blk"), None)
    row = P(("dp", "blk"))
    packs = P(None, "dp", "blk", None)
    parameters = (rows, row, rows, row, row, row, rows, row, rows, row, row, row)
    return jax.shard_map(
        functools.partial(per_device, (mesh.shape["dp"], mesh.shape["blk"])),
        mesh=mesh,
        in_specs=(packs, P(None, "dp", None)) + parameters + (packs,),
        out_specs=(packs, packs) + parameters,
        check_vma=False,
    )
```

```python
import functools
import math

import jax
import jax.numpy as jnp
from jax import lax
from jax.experimental import pallas as pl
from jax.experimental.pallas import tpu as pltpu
from jax.sharding import PartitionSpec as P

H = 12
HD = 64
NEGATIVE = -1e30
EPSILON = 1e-05
MESH = pl.DeviceIdType.MESH
BF16 = jnp.bfloat16
F32 = jnp.float32

VECTOR_TILE = (8, 128)


def place():
    dp = lax.axis_index("dp")
    blk = lax.axis_index("blk")
    return dp // 2, dp % 2, blk // 2, blk % 2


def device(z, y, x, c):
    return (z * 2 + y, x * 2 + c)


def signal(peers):
    barrier = pltpu.get_barrier_semaphore()
    for peer in peers:
        pl.semaphore_signal(barrier, inc=1, device_id=peer, device_id_type=MESH)


def arrived(peers):
    pl.semaphore_wait(pltpu.get_barrier_semaphore(), len(peers))


def neighbours(zs):
    z, y, x, c = place()
    sib = device(z, y, x, 1 - c)
    xpeer = device(z, y, 1 - x, c)
    ypeer = device(z, 1 - y, x, c)
    zpeers = [device((z + k) % zs, y, x, c) for k in range(1, zs)]
    return sib, xpeer, ypeer, zpeers


def remote(src, dst, sems, index, peer):
    send, recv = sems
    return pltpu.make_async_remote_copy(
        src_ref=src,
        dst_ref=dst,
        send_sem=send.at[index],
        recv_sem=recv.at[index],
        device_id=peer,
        device_id_type=MESH,
    )


def pick(c, first, second):
    return first + c * (second - first)


class Links:
    def __init__(self, zs):
        self.zs = zs
        self.z, self.y, self.x, self.c = z, y, x, c = place()
        self.sib, self.xpeer, self.ypeer, self.zpeers = neighbours(zs)
        self.pz, self.fz = z + 1 - 2 * (z % 2), (z + 2) % zs
        self.pfz = (self.pz + 2) % zs
        self.partner = device(self.pz, y, x, c)
        self.far = device(self.fz, y, x, c)
        self.mix = (
            tuple(pick(c, a, b) for a, b in zip(self.xpeer, self.ypeer)),
            tuple(pick(c, a, b) for a, b in zip(self.ypeer, self.xpeer)),
            (pick(c, y, 1 - y), pick(c, 1 - x, x)),
            (pick(c, 1 - y, y), pick(c, x, 1 - x)),
        )
        self.over_y = (self.ypeer, self.xpeer, (1 - y, x), (y, 1 - x))
        self.over_x = (self.xpeer, self.ypeer, (y, 1 - x), (1 - y, x))


class Again:
    def __init__(self, make):
        self.make = make

    def start(self):
        self.make().start()

    def wait_recv(self):
        self.make().wait_recv()

    def wait_send(self):
        self.make().wait_send()

    def wait(self):
        self.make().wait()


class Mover:
    def __init__(self, links, sems, row):
        self.l, self.sems, self.row = links, sems, row
        self.started = []

    def sent(self, index, src, dst, peer):
        copy = Again(lambda: remote(src(), dst(), self.sems, (self.row, index), peer))
        self.started.append(copy)
        return copy

    def send(self, index, src, dst, peer):
        copy = self.sent(index, src, dst, peer)
        copy.start()
        return copy

    def hand(self, index, ref, peer):
        return self.send(index, ref, ref, peer)

    def drain(self):
        for copy in self.started:
            copy.wait_send()
        self.started = []


class GatherZFirst(Mover):
    def __init__(self, links, sems, row, block, column, mode, two=False):
        super().__init__(links, sems, row)
        self.block, self.column, self.mode, self.two = block, column, mode, two

    def start(self):
        l = self.l
        own = lambda: self.block(l.z, l.y, l.x)
        if self.two:
            self.tf = self.hand(1, own, l.far)
            self.zc = [self.hand(0, own, l.partner)]
        else:
            self.zc = [self.hand(k, own, peer) for k, peer in enumerate(l.zpeers)]

    def relay(self):
        l = self.l
        self.tf.wait_recv()
        self.zc.append(self.hand(2, lambda: self.block(l.fz, l.y, l.x), l.partner))

    def columns(self):
        l, b = self.l, self.l.zs - 1
        for copy in self.zc:
            copy.wait_recv()
        own = lambda: self.column(l.y, l.x)
        self.tx = self.hand(b, own, l.xpeer)
        self.ty = self.hand(b + 1, own, l.ypeer)
        self.shares = [self.hand(b + 3, own, l.sib)]

    def forward(self):
        l, b = self.l, self.l.zs - 1
        self.tx.wait_recv()
        if self.mode == "y":
            to, _, _, (fy, fx) = l.over_y
        else:
            self.ty.wait_recv()
            to, _, _, (fy, fx) = l.mix
        self.fw = self.hand(b + 2, lambda: self.column(fy, fx), to)
        self.shares.append(self.hand(b + 4, lambda: self.column(l.y, 1 - l.x), l.sib))
        if self.mode != "y":
            self.share_y()

    def share_y(self):
        l, b = self.l, self.l.zs - 1
        self.shares.append(self.hand(b + 5, lambda: self.column(1 - l.y, l.x), l.sib))

    def last(self):
        l, b = self.l, self.l.zs - 1
        if self.mode == "y":
            self.ty.wait_recv()
            self.share_y()
        self.fw.wait_recv()
        self.shares.append(self.hand(b + 6, lambda: self.column(1 - l.y, 1 - l.x), l.sib))

    def finish(self):
        for copy in self.shares:
            copy.wait_recv()


class GatherZLast(Mover):
    def __init__(self, links, sems, row, block, plane):
        super().__init__(links, sems, row)
        self.block, self.plane = block, plane

    def start(self):
        l = self.l
        own = lambda: self.block(l.z, l.y, l.x)
        self.tx = self.hand(0, own, l.xpeer)
        self.ty = self.hand(1, own, l.ypeer)

    def forward(self):
        l = self.l
        self.tx.wait_recv()
        self.ty.wait_recv()
        to, _, _, (fy, fx) = l.mix
        self.fw = self.hand(2, lambda: self.block(l.z, fy, fx), to)

    def planes(self):
        l = self.l
        self.fw.wait_recv()
        own = lambda: self.plane(l.z)
        self.tf = self.hand(4, own, l.far)
        self.tp = self.hand(3, own, l.partner)
        self.shares = [self.hand(2 + l.zs, own, l.sib)]

    def share(self, k, z):
        self.shares.append(self.hand(3 + self.l.zs + k, lambda: self.plane(z), self.l.sib))

    def relay(self):
        l = self.l
        self.tf.wait_recv()
        self.tr = self.hand(5, lambda: self.plane(l.fz), l.partner)
        self.share(1, l.fz)

    def last(self):
        l = self.l
        self.tp.wait_recv()
        self.share(0, l.pz)
        self.tr.wait_recv()
        self.share(2, l.pfz)

    finish = GatherZFirst.finish


def add_into(ref, *others):
    total = ref[...].astype(F32)
    for other in others:
        total = total + other[...].astype(F32)
    ref[...] = total.astype(ref.dtype)


class ScatterZFirst(Mover):
    def __init__(self, links, sems, row, sums, bufs, own, over, two=False):
        super().__init__(links, sems, row)
        self.block, self.column = sums
        self.diag, self.n3, self.n2, self.zb = bufs
        self.own = own
        self.over = over
        self.two = two

    def add_sib(self, waits):
        l = self.l
        for copy in waits:
            copy.wait_recv()

        def body(n, carry):
            at = (n // 4, (n // 2) % 2, n % 2)
            add_into(self.block(*at), self.own(*at))
            return carry

        steps(4 * l.zs, body)
        peer3, peer2, (y3, x3), (y2, x2) = self.over
        self.c3 = self.send(0, lambda: self.column(1 - l.y, 1 - l.x), lambda: self.diag, peer3)
        self.cn = self.send(1, lambda: self.column(y3, x3), lambda: self.n3, peer3)

    def piece(self, n):
        l = self.l
        peer3, peer2, (y3, x3), (y2, x2) = self.over
        for index, (by, bx), to in ((0, (1 - l.y, 1 - l.x), self.diag), (1, (y3, x3), self.n3)):
            remote(
                self.block(n, by, bx), to.at[n], self.sems, (self.row, index), peer3
            ).start()

    def pieces(self):
        l = self.l
        peer3, peer2, (y3, x3), (y2, x2) = self.over
        self.c3 = self.sent(
            0, lambda: self.column(1 - l.y, 1 - l.x), lambda: self.diag, peer3
        )
        self.cn = self.sent(1, lambda: self.column(y3, x3), lambda: self.n3, peer3)

    def add_diag(self):
        l = self.l
        peer3, peer2, (y3, x3), (y2, x2) = self.over
        self.c3.wait_recv()

        def body(n, carry):
            add_into(self.block(n, y2, x2), self.diag.at[n])
            return carry

        steps(l.zs, body)
        self.c2 = self.send(2, lambda: self.column(y2, x2), lambda: self.n2, peer2)

    def add_near(self):
        l = self.l
        self.cn.wait_recv()
        self.c2.wait_recv()

        def body(n, carry):
            add_into(self.block(n, l.y, l.x), self.n3.at[n], self.n2.at[n])
            return carry

        steps(l.zs, body)
        if self.two:
            self.cp = self.send(
                4, lambda: self.block(l.pfz, l.y, l.x), lambda: self.zb.at[1], l.partner
            )
            self.zc = [
                self.send(
                    3, lambda: self.block(l.pz, l.y, l.x), lambda: self.zb.at[0], l.partner
                )
            ]
        else:
            self.zc = [
                self.send(
                    3 + k,
                    lambda k=k: self.block((l.z + k + 1) % l.zs, l.y, l.x),
                    lambda k=k: self.zb.at[k],
                    peer,
                )
                for k, peer in enumerate(l.zpeers)
            ]

    def add_far(self):
        l = self.l
        self.cp.wait_recv()
        add_into(self.block(l.fz, l.y, l.x), self.zb.at[1])
        self.zc.append(
            self.send(5, lambda: self.block(l.fz, l.y, l.x), lambda: self.zb.at[2], l.far)
        )

    def total(self):
        l = self.l
        for copy in self.zc:
            copy.wait_recv()
        total = self.block(l.z, l.y, l.x)[...].astype(F32)
        for k in (0, 2) if self.two else range(l.zs - 1):
            total = total + self.zb[k].astype(F32)
        return total


class ScatterZLast(Mover):
    def __init__(self, links, sems, row, sums, bufs, own, over):
        super().__init__(links, sems, row)
        self.block, self.plane = sums
        self.diag, self.n3, self.n2, self.zb = bufs
        self.own = own
        self.over = over

    def piece(self, n):
        l = self.l
        for k, at in ((0, l.pz), (1, l.pfz)):

            @pl.when(at == n)
            def _(k=k):
                remote(
                    self.plane(n), self.zb.at[k], self.sems, (self.row, 3 + k), l.partner
                ).start()

    def pieces(self):
        l = self.l
        self.zc = [self.sent(3, lambda: self.plane(l.pz), lambda: self.zb.at[0], l.partner)]
        self.cp = self.sent(4, lambda: self.plane(l.pfz), lambda: self.zb.at[1], l.partner)

    def add_far(self):
        l = self.l
        self.cp.wait_recv()

        def body(n, carry):
            by, bx = n // 2, n % 2
            add_into(self.block(l.fz, by, bx), self.zb.at[1, by, bx])
            return carry

        steps(4, body)
        self.zc.append(
            self.send(5, lambda: self.plane(l.fz), lambda: self.zb.at[2], l.far)
        )

    def add_planes(self):
        l = self.l
        for copy in self.zc:
            copy.wait_recv()

        def body(n, carry):
            by, bx = n // 2, n % 2
            add_into(
                self.block(l.z, by, bx), *[self.zb.at[k, by, bx] for k in (0, 2)]
            )
            return carry

        steps(4, body)
        peer3, peer2, (y3, x3), (y2, x2) = self.over
        self.c3 = self.send(0, lambda: self.block(l.z, 1 - l.y, 1 - l.x), lambda: self.diag, peer3)
        self.cn = self.send(1, lambda: self.block(l.z, y3, x3), lambda: self.n3, peer3)

    def add_diag(self):
        l = self.l
        peer3, peer2, (y3, x3), (y2, x2) = self.over
        self.c3.wait_recv()
        add_into(self.block(l.z, y2, x2), self.diag)
        self.c2 = self.send(2, lambda: self.block(l.z, y2, x2), lambda: self.n2, peer2)

    def total(self):
        l = self.l
        self.cn.wait_recv()
        self.c2.wait_recv()
        own = self.block(l.z, l.y, l.x)[...].astype(F32)
        return own + self.n3[...].astype(F32) + self.n2[...].astype(F32)


def steps(count, body):
    lax.fori_loop(0, count, body, 0)


def once(body):
    lax.fori_loop(0, 1, lambda n, carry: (body(), carry)[1], 0)


def dot(left, right):
    return jnp.dot(left, right, preferred_element_type=F32)


def dot_t(left, right):
    return lax.dot_general(left, right, (((1,), (1,)), ((), ())), preferred_element_type=F32)


def t_dot(left, right):
    return lax.dot_general(left, right, (((0,), (0,)), ((), ())), preferred_element_type=F32)


def lanes(shape):
    return lax.broadcasted_iota(jnp.int32, shape, len(shape) - 1)


def rows_of(shape):
    return lax.broadcasted_iota(jnp.int32, shape, len(shape) - 2)


def turn(part, cosine, sine, direction):
    swapped = jnp.where(
        lanes(part.shape) % HD < HD // 2,
        pltpu.roll(part, 128 - HD // 2, 1),
        pltpu.roll(part, HD // 2, 1),
    )
    return part * cosine + (direction * swapped) * sine


def rows_mean(values):
    return jnp.sum(values, axis=-1, keepdims=True) * (1.0 / values.shape[-1])


def selection(share, columns):
    shape = (VECTOR_TILE[1], columns)
    column = lanes(shape).astype(F32)
    owner = jnp.floor((column + 0.5) * (1.0 / share))
    within = (column - owner * share).astype(jnp.int32)
    return jnp.where(rows_of(shape) == within, 1.0, 0.0).astype(BF16)


def owned(share, start, columns, devices):
    shape = (devices, columns)
    first = rows_of(shape) * share
    column = lanes(shape) + start
    return (column >= first) & (column < first + share)


PAIRS = 2
MODES = dict(
    gJ0="mix",
    gJ1="mix",
    gJ2="y",
    gO="mix",
    gE0="mix",
    gE1="mix",
    gR1="mix",
    sR1="mix",
    sR2="y",
    sE="mix",
    sO="mix",
    sJ0="x",
    sJ1="y",
    sJ2="x",
    sV="y",
)
FIRST_COPIES = ("V", "R2", "tok")
GATHER_ORDER = (
    (
        "gE0.start", "gV.columns", "gR1.start", "gJ0.columns",
        "gE1.start", "gJ1.columns", "gV.forward", "gJ0.forward",
        "gO.columns", "gE0.relay", "gJ1.forward", "tables.make",
        "gJ2.columns", "gV.last", "gJ0.last", "gV.finish",
    ),
    ("gE1.relay", "gR1.relay", "gE0.columns", "gR2.planes", "gO.forward"),
    ("gJ2.forward", "gE1.columns", "gJ1.last"),
    ("gO.last", "gR1.columns", "gJ2.last"),
    ("gE0.forward", "gR2.relay"),
    ("gE1.forward", "gO.finish", "gR1.forward"),
    ("cot.start", "gE0.last"),
    ("gR2.last", "gE1.last", "gE0.finish"),
    ("gR1.last", "gE1.finish"),
    ("gR2.finish", "gR1.finish"),
)
SCATTER_ORDER = (
    ("sR1.add_diag", "sE.add_sib"),
    (),
    ("sR2.add_far", "sR1.add_near"),
    ("sE.add_diag",),
    ("sO.add_sib",),
    ("sR1.add_far",),
    ("sO.add_diag", "sJ0.add_sib", "sJ1.add_sib", "sE.add_near"),
    ("sR2.add_planes",),
    ("sO.add_near", "sJ1.add_diag", "sJ0.add_diag", "sJ2.add_sib", "sE.add_far"),
    (
        "sJ1.add_near", "sV.add_sib", "sR2.add_diag", "sJ2.add_diag",
        "sJ0.add_near", "sV.add_diag", "gx.go", "sJ2.add_near",
    ),
    ("sV.add_near",),
    (),
    ("yex.go",),
)
JOINT_B, OUTPUT_B, GAIN1, SHIFT1, EXPAND_B, REDUCE_B, GAIN2, SHIFT2 = range(8)


def layer_kernel(zs, widths, lens, jw, ow, ew, rw, tok, cot, *rest):
    vecs, rest = rest[:8], rest[8:]
    (y_out, far_in, *results), rest = rest[:7], rest[7:]
    (gj, go, ge, gr, gv), rest = rest[:5], rest[5:]
    ready = {
        name: Again(lambda n=n, held=held: pltpu.make_async_copy(held, results[n], result_sems.at[n]))
        for n, (name, held) in enumerate(dict(gj=gj, go=go, ge=ge, gr=gr, gv=gv).items())
    }
    (J, O, E, R, V, T), rest = rest[:6], rest[6:]
    (stage_j, stage_o, stage_e, pair_j, pair_o, pair_e), rest = rest[:6], rest[6:]
    (cos_t, sin_t, QKV, PR, ATT, X1, I1, HL, FX, DRED, COT, BIAS, GVEC), rest = (
        rest[:13],
        rest[13:],
    )
    (SR, SE, SO, SJ, SV, r1_bufs, r2_bufs, e_bufs, o_bufs, j_bufs, v_bufs, VG), rest = (
        rest[:12],
        rest[12:],
    )
    (
        pair_sems,
        gather_sems,
        tok_sems,
        cot_sems,
        y_sems,
        far_sems,
        first_sems,
        scatter_sems,
        last_sems,
        local_sems,
        result_sems,
    ) = rest
    l = Links(zs)
    z, y, x, c = l.z, l.y, l.x, l.c
    micro, shard, width = ATT.shape
    own_rows = micro * shard
    ff = zs * 8 * rw.shape[0]
    devices = zs * 8
    pack = micro * shard
    full = [w * devices for w in widths]
    sets = width // (128 * PAIRS)
    part = 128 * PAIRS
    hp = 3 * part // 2
    kinds = sorted(set(full))
    sel_at = [sum(k for k in kinds if k < f) for f in full]
    sel_shape = pltpu.VMEM((VECTOR_TILE[1], sum(kinds)), BF16)

    blk = x * 2 + c
    others = [(blk + k) % micro for k in range(1, micro)]

    def exchange(sems, src, dst):
        return [
            Again(
                lambda k=k, b=b: remote(src.at[b], dst.at[blk], sems, k, (l.z * 2 + l.y, b))
            )
            for k, b in enumerate(others)
        ]

    tok_ex = exchange(tok_sems, tok, T)
    cot_ex = exchange(cot_sems, cot, COT)
    y_ex = exchange(y_sems, COT, y_out)
    far_ex = exchange(far_sems, DRED, far_in)
    keep_tok = pltpu.make_async_copy(tok.at[blk], T.at[blk], local_sems.at[0])
    keep_cot = pltpu.make_async_copy(cot.at[blk], COT.at[blk], local_sems.at[1])
    keep_y = Again(lambda: pltpu.make_async_copy(COT.at[blk], y_out.at[blk], local_sems.at[2]))
    keep_far = Again(lambda: pltpu.make_async_copy(DRED.at[blk], far_in.at[blk], local_sems.at[3]))
    keep_tok.start()
    keep_cot.start()
    peers = [(l.z * 2 + l.y, b) for b in others] + [l.ypeer] + l.zpeers
    signal(peers)

    def halves(ref):
        return (
            lambda bz, by, bx: ref.at[c, bz, by, bx],
            lambda by, bx: ref.at[c, :, by, bx],
        )

    def natural(ref):
        return (
            lambda bz, by, bx: ref.at[bz, by, bx, c],
            lambda by, bx: ref.at[:, by, bx, c],
        )

    split = rw.shape[0] // 3
    low, high = pl.ds(0, split), pl.ds(split, rw.shape[0] - split)
    gV = GatherZFirst(l, gather_sems, 0, *natural(V), "mix")
    gO = GatherZFirst(l, gather_sems, 1, *halves(O), MODES["gO"])
    gE = [
        GatherZFirst(
            l,
            gather_sems,
            row,
            lambda bz, by, bx, cols=cols: E.at[c, bz, by, bx, :, cols],
            lambda by, bx, cols=cols: E.at[c, :, by, bx, :, cols],
            MODES["gE%d" % n],
            two=True,
        )
        for n, (row, cols) in enumerate(
            ((2, pl.ds(0, E.shape[5] // 2)), (5 + sets, pl.ds(E.shape[5] // 2, E.shape[5] // 2)))
        )
    ]
    gR1 = GatherZFirst(
        l,
        gather_sems,
        3,
        lambda bz, by, bx: R.at[bz, by, bx, c, low],
        lambda by, bx: R.at[:, by, bx, c, low],
        MODES["gR1"],
        two=True,
    )
    gR2 = GatherZLast(
        l,
        gather_sems,
        4,
        lambda bz, by, bx: R.at[bz, by, bx, c, high],
        lambda bz: R.at[bz, :, :, c, high],
    )
    gJ = [
        GatherZFirst(l, gather_sems, 5 + g, *halves(J.at[g]), MODES["gJ%d" % g])
        for g in range(sets)
    ]
    for g in range(sets):
        q, k, v = (n * width + g * part for n in range(3))
        at = g * hp
        stage_j[0, :, at : at + part] = jw[:, q : q + part].astype(F32)
        stage_j[0, :, at + part : at + hp] = jw[:, k : k + hp - part].astype(F32)
        stage_j[1, :, at : at + hp - part] = jw[:, k + hp - part : k + part].astype(F32)
        stage_j[1, :, at + hp - part : at + hp] = jw[:, v : v + part].astype(F32)
    for w, stage in ((ow, stage_o), (ew, stage_e)):
        half = stage.shape[2]
        stage[0] = w[:, :half].astype(F32)
        stage[1] = w[:, half:].astype(F32)
    R[z, y, x, c] = rw[...]
    V[z, y, x, c] = jnp.zeros(VECTOR_TILE, F32)
    for i, share in enumerate(widths):
        V[z, y, x, c, i : i + 1, :share] = vecs[i][...].astype(F32)
    arrived(peers)
    pairs = []
    for i, (stage, pair) in enumerate(
        ((stage_j, pair_j), (stage_o, pair_o), (stage_e, pair_e))
    ):
        copy = remote(stage.at[1 - c], pair, pair_sems, i, l.sib)
        copy.start()
        pairs.append(copy)
    begin = dict(
        R2=gR2.start,
        V=gV.start,
        tok=lambda: [copy.start() for copy in tok_ex],
        cot=lambda: [copy.start() for copy in cot_ex],
    )
    for name in FIRST_COPIES:
        begin[name]()

    def pair_up(W, mine, other):
        first = jnp.where(c == 0, mine, other)
        second = jnp.where(c == 0, other, mine)
        W[c, z, y, x] = jnp.concatenate([first, second], axis=0).astype(BF16)

    pairs[0].wait_recv()
    for g in range(sets):
        at = slice(g * hp, (g + 1) * hp)
        pair_up(J.at[g], stage_j[c, :, at], pair_j[:, at])
        gJ[g].start()
    pairs[1].wait_recv()
    pair_up(O, stage_o[c], pair_o[...])
    gO.start()
    pairs[2].wait_recv()
    pair_up(E, stage_e[c], pair_e[...])
    gR2.forward()

    ends = []
    for j in range(lens.shape[1]):
        ends.append(lens[blk, j] + (ends[-1] if ends else 0))
    exponent = (lanes((1, 128)) % (HD // 2)).astype(F32)
    frequency = jnp.exp(exponent * (-2.0 * math.log(10000.0) / HD))

    def tables(b, carry):
        position = b * shard + rows_of((shard, 128))
        begin = jnp.zeros((shard, 128), jnp.int32)
        for end in ends:
            begin = jnp.where(position >= end, end, begin)
        angle = (position - begin).astype(F32) * frequency
        cos_t[b] = jnp.cos(angle)
        sine = jnp.sin(angle)
        sin_t[b] = jnp.where(lanes((shard, 128)) % HD < HD // 2, -sine, sine)
        query_at = b * shard + rows_of((shard, pack))
        key_at = lanes((shard, pack))
        query_seg = jnp.zeros((shard, pack), jnp.int32)
        key_seg = jnp.zeros((shard, pack), jnp.int32)
        for end in ends:
            query_seg = query_seg + (query_at >= end).astype(jnp.int32)
            key_seg = key_seg + (key_at >= end).astype(jnp.int32)
        FX[b, :, :pack] = jnp.where(query_seg == key_seg, 0.0, NEGATIVE)
        return carry

    gather_at = GATHER_ORDER
    do = dict(
        gV=gV,
        gO=gO,
        gE0=gE[0],
        gE1=gE[1],
        gR1=gR1,
        gR2=gR2,
    )
    for g in range(sets):
        do["gJ%d" % g] = gJ[g]

    def run(order):
        for step in order:
            name, what = step.split(".")
            getattr(do[name], what)()

    class Tables:
        def make(self):
            steps(micro, tables)

    class Cotangent:
        def start(self):
            for copy in cot_ex:
                copy.start()

    do["tables"] = Tables()
    do["cot"] = Cotangent()
    run(gather_at[0])
    GVEC[...] = jnp.zeros_like(GVEC)

    def selections(SEL):
        for kind in kinds:
            at = sel_at[full.index(kind)]
            SEL[:, at : at + kind] = selection(kind // devices, kind)

    def chosen(SEL, i, start):
        return SEL[:, sel_at[i] + start : sel_at[i] + start + width]

    def unpack(SEL):
        selections(SEL)
        for i, share in enumerate(widths):
            packed = V[:, :, :, :, i, :].reshape(devices, VECTOR_TILE[1]).astype(BF16)
            for start in range(0, full[i], width):
                spread = dot(packed, chosen(SEL, i, start))
                mine = jnp.where(owned(share, start, width, devices), spread, 0.0)
                BIAS[i : i + 1, start : start + width] = jnp.sum(mine, axis=0, keepdims=True)

    def pack_grads(SEL):
        selections(SEL)
        for i, share in enumerate(widths):
            total = jnp.zeros((devices, VECTOR_TILE[1]), F32)
            for start in range(0, full[i], width):
                line = GVEC[i : i + 1, start : start + width]
                high_part = line.astype(BF16).astype(F32)
                low_part = line - high_part
                keep = owned(share, start, width, devices)
                for piece in (high_part, low_part):
                    total = total + dot_t(
                        jnp.where(keep, piece, 0.0).astype(BF16), chosen(SEL, i, start)
                    )
            VG[:, :, :, :, i, :] = total.reshape(zs, 2, 2, 2, VECTOR_TILE[1])

    def bias(i, start=0, size=None):
        size = full[i] if size is None else size
        return BIAS[i : i + 1, pl.ds(start, size)]

    def flat(ref, *index):
        value = ref[index]
        return value.reshape((-1, value.shape[-1]))

    def wide(ref, h, start, size):
        return ref[h, :, :, :, :, pl.ds(start, size)].reshape(-1, size)

    def rotated(values, cosine, sine, direction):
        parts = []
        for n in range(values.shape[1] // 128):
            parts.append(turn(values[:, n * 128 : (n + 1) * 128], cosine, sine, direction))
        return jnp.concatenate(parts, axis=1)

    def set_weights(g):
        return jnp.concatenate([wide(J.at[g], 0, 0, hp), wide(J.at[g], 1, 0, hp)], axis=1)

    def project(g):
        value = dot(T[...].reshape(own_rows, width), set_weights(g))
        value = value + jnp.concatenate(
            [bias(JOINT_B, n * width + g * part, part) for n in range(3)], axis=1
        )
        cosine, sine = cos_t[...].reshape(pack, 128), sin_t[...].reshape(pack, 128)
        q = rotated(value[:, :part], cosine, sine, 1.0).astype(BF16)
        q = q * jnp.asarray(HD ** (-0.5), BF16)
        k = rotated(value[:, part : 2 * part], cosine, sine, 1.0).astype(BF16)
        v = value[:, 2 * part :].astype(BF16)
        for n, piece in enumerate((q, k, v)):
            at = (3 * g + n) * part
            QKV[:, :, at : at + part] = piece.reshape(micro, shard, part)

    pl.run_scoped(unpack, sel_shape)
    keep_tok.wait()
    for copy in tok_ex:
        copy.wait_recv()
    oh = O.shape[5]

    first_head = lanes((shard, 128)) < HD

    def stacked(two):
        zero = jnp.zeros_like(two)
        return jnp.concatenate(
            [jnp.where(first_head, two, zero), jnp.where(first_head, zero, two)], axis=0
        )

    def unstacked(two):
        return jnp.where(first_head, two[:shard], two[shard:])

    def pair_at(g, i):
        starts = [(3 * g + n) * part + i * 128 for n in range(3)] + [g * part + i * 128]
        return [pl.ds(pl.multiple_of(at, 128), 128) for at in starts]

    def attend(g):
        def pair(i, carry):
            q_at, k_at, v_at, o_at = pair_at(g, i)
            k = QKV[:, :, k_at].reshape(pack, 128)
            v = QKV[:, :, v_at].reshape(pack, 128)
            for m in range(micro):
                scores = dot_t(stacked(QKV[m, :, q_at]), k)
                mask = FX[m, :, :pack]
                scores = scores + jnp.concatenate([mask, mask], axis=0)
                weights = jnp.exp(scores - jnp.max(scores, axis=-1, keepdims=True))
                prob = weights * (1.0 / jnp.sum(weights, axis=-1, keepdims=True))
                prob = prob.astype(BF16)
                PR[g, i, m] = prob
                ATT[m, :, o_at] = unstacked(dot(prob, v)).astype(BF16)
            return carry

        steps(PAIRS, pair)

    for g in range(sets):
        gJ[g].finish()
        once(functools.partial(project, g))
        run(gather_at[1 + 2 * g])
        attend(g)
        run(gather_at[2 + 2 * g])

    def output():
        attended = ATT[...].reshape(own_rows, width)
        FX[:, :, :oh] = dot(attended, wide(O, 0, 0, oh)).reshape(micro, shard, oh)
        FX[:, :, oh:] = dot(attended, wide(O, 1, 0, oh)).reshape(micro, shard, oh)

    def first_norm(m, carry):
        residual = T[m].astype(F32) + (FX[m] + bias(OUTPUT_B))
        centered = residual - rows_mean(residual)
        inverse = lax.rsqrt(rows_mean(centered * centered) + EPSILON)
        normal = centered * inverse
        X1[m] = normal
        I1[m] = jnp.broadcast_to(inverse, (shard, 128))
        HL[m] = (normal * bias(GAIN1) + bias(SHIFT1)).astype(BF16)
        return carry

    once(output)
    steps(micro, first_norm)
    run(gather_at[1 + 2 * sets])
    tile = ff // zs
    per_half = zs // 2
    hidden_low = lambda: HL[...].reshape(own_rows, width)

    def sums(ref):
        return (lambda bz, by, bx: ref.at[bz, by, bx]), (lambda by, bx: ref.at[:, by, bx])

    def own_half(ref):
        return lambda bz, by, bx: ref.at[c, bz, by, bx]

    def over(name):
        return dict(y=l.over_y, x=l.over_x, mix=l.mix)[MODES[name]]

    sR1 = ScatterZFirst(
        l,
        scatter_sems,
        0,
        (
            lambda bz, by, bx: SR.at[bz, by, bx, low],
            lambda by, bx: SR.at[:, by, bx, low],
        ),
        r1_bufs,
        lambda bz, by, bx: R.at[bz, by, bx, c, low],
        over("sR1"),
        two=True,
    )
    sR2 = ScatterZLast(
        l,
        scatter_sems,
        1,
        (lambda bz, by, bx: SR.at[bz, by, bx, high], lambda bz: SR.at[bz, :, :, high]),
        r2_bufs,
        lambda bz, by, bx: R.at[bz, by, bx, c, high],
        over("sR2"),
    )
    sE = ScatterZFirst(
        l, scatter_sems, 2, sums(SE), e_bufs, own_half(E), over("sE"), two=True
    )
    sO = ScatterZFirst(l, scatter_sems, 3, sums(SO), o_bufs, own_half(O), over("sO"))
    sV = ScatterZFirst(
        l,
        scatter_sems,
        4,
        sums(SV),
        v_bufs,
        lambda bz, by, bx: VG.at[bz, by, bx, c],
        over("sV"),
    )
    firstR = [
        Again(lambda n=n: remote(R.at[n, :, :, 1 - c], SR.at[n], first_sems, (0, n), l.sib))
        for n in range(zs)
    ]
    firstE = Again(lambda: remote(E.at[c], SE, first_sems, (1, 0), l.sib))
    firstO = Again(lambda: remote(O.at[1 - c], SO, first_sems, (2, 0), l.sib))
    firstV = Again(
        lambda: remote(VG.at[:, :, :, 1 - c], SV, first_sems, (3, 0), l.sib)
    )
    def feed_forward(GP):
        pl.run_scoped(functools.partial(through, GP), pltpu.VMEM((micro, shard, ff), BF16))
        pl.run_scoped(functools.partial(expand_gradient, GP), pltpu.VMEM(E.shape[1:], BF16))

    def through(GP, ACT):
        def expand(step, carry):
            h, t = step % 2, step // 2
            n = h * per_half + t

            @pl.when(step == zs // 2)
            def _():
                run(gather_at[2 + 2 * sets])

            to = pl.ds(pl.multiple_of(n * tile, 128), tile)
            weight = E[h, :, :, :, :, pl.ds(pl.multiple_of(t * tile, 128), tile)]
            value = dot(hidden_low(), weight.reshape(width, tile)) + BIAS[
                EXPAND_B : EXPAND_B + 1, to
            ]
            scale = math.sqrt(2.0 / math.pi)
            square = value * value
            t_value = jnp.tanh(value * (scale + (scale * 0.044715) * square))
            half = 0.5 * (1.0 + t_value)
            ACT[:, :, to] = (value * half).astype(BF16).reshape(micro, shard, tile)
            slope = half + value * (0.5 * (1.0 - t_value * t_value)) * (
                scale + (3.0 * scale * 0.044715) * square
            )
            GP[:, :, to] = slope.astype(BF16).reshape(micro, shard, tile)
            return carry

        steps(zs, expand)
        run(gather_at[3 + 2 * sets])

        chunk = 2

        def reduce(n, carry):
            at = pl.ds(n * chunk, chunk)
            reduced = dot(ACT[at].reshape(chunk * shard, ff), R[...].reshape(ff, width))
            FX[at] = reduced.reshape(chunk, shard, width)
            return carry

        def second_norm(n, carry):
            at = pl.ds(n * chunk, chunk)
            rows = lambda ref: ref[at].reshape(chunk * shard, width)
            hidden = rows(X1) * bias(GAIN1) + bias(SHIFT1)
            residual = hidden + (rows(FX) + bias(REDUCE_B))
            centered = residual - rows_mean(residual)
            inverse = lax.rsqrt(rows_mean(centered * centered) + EPSILON)
            normal = centered * inverse
            result = (normal * bias(GAIN2) + bias(SHIFT2)).astype(BF16)
            seed = rows(COT).astype(F32)
            COT[at] = result.reshape(chunk, shard, width)
            GVEC[GAIN2 : GAIN2 + 1, :width] += jnp.sum(seed * normal, axis=0, keepdims=True)
            GVEC[SHIFT2 : SHIFT2 + 1, :width] += jnp.sum(seed, axis=0, keepdims=True)
            dn = seed * bias(GAIN2)
            grad = inverse * (dn - rows_mean(dn) - normal * rows_mean(dn * normal))
            FX[at] = grad.reshape(chunk, shard, width)
            grad_low = grad.astype(BF16)
            DRED[at] = grad_low.reshape(chunk, shard, width)
            GVEC[REDUCE_B : REDUCE_B + 1, :width] += jnp.sum(
                grad_low.astype(F32), axis=0, keepdims=True
            )
            if "yex.go" in SCATTER_ORDER[12]:
                for copy, b in zip(y_ex, others):
                    pl.when(b // chunk == n)(copy.start)
            return carry

        steps(micro // chunk, reduce)
        keep_cot.wait()
        for copy in cot_ex:
            copy.wait_recv()
        steps(micro // chunk, second_norm)
        keep_y.start()
        for item in [gV, gO, gR1, gR2] + gE + gJ:
            item.drain()
        for copy in pairs + tok_ex + cot_ex:
            copy.wait_send()

        def back_reduce(n, carry):
            at = pl.ds(pl.multiple_of(n * tile, 128), tile)
            dred = DRED[...].reshape(own_rows, width)
            grad = dot_t(dred, flat(R, n))
            grad = grad * GP[:, :, at].reshape(own_rows, tile).astype(F32)
            grad_low = grad.astype(BF16)
            GP[:, :, at] = grad_low.reshape(micro, shard, tile)
            GVEC[EXPAND_B : EXPAND_B + 1, at] = jnp.sum(
                grad_low.astype(F32), axis=0, keepdims=True
            )
            weight_grad = t_dot(ACT[:, :, at].reshape(own_rows, tile), dred)
            R[n] = weight_grad.astype(BF16).reshape(R.shape[1:])

            first_reduce(n).start()
            pl.when(n > 0)(functools.partial(pass_on, n - 1))
            return carry

        steps(zs, back_reduce)

    def expand_gradient(GP, GE):
        def back_expand(half, h, t, carry):
            at = pl.ds(pl.multiple_of((h * per_half + t) * tile, 128), tile)
            grad = t_dot(hidden_low(), GP[:, :, at].reshape(own_rows, tile))
            half[:, :, :, :, pl.ds(pl.multiple_of(t * tile, 128), tile)] = grad.astype(
                BF16
            ).reshape(zs, 2, 2, E.shape[4], tile)
            return carry

        def back_hidden():
            for h in range(2):
                some = pl.ds(h * (ff // 2), ff // 2)
                FX[...] += dot_t(
                    GP[:, :, some].reshape(own_rows, ff // 2), wide(E, h, 0, ff // 2)
                ).reshape(micro, shard, width)

        to_sib = remote(GE, SE, first_sems, (1, 0), l.sib)
        steps(per_half, functools.partial(back_expand, GE, 1 - c))
        to_sib.start()
        once(functools.partial(pass_last))
        once(back_hidden)
        steps(per_half, functools.partial(back_expand, E.at[c], c))
        to_sib.wait_send()

    def first_reduce(n):
        return remote(R.at[n, :, :, 1 - c], SR.at[n], first_sems, (0, n), l.sib)

    def pass_on(n):
        first_reduce(n).wait_recv()
        add_into(SR.at[n], R.at[n, :, :, c])
        sR1.piece(n)
        sR2.piece(n)

    def pass_last():
        pass_on(zs - 1)
        sR1.pieces()
        sR2.pieces()

    pl.run_scoped(feed_forward, pltpu.VMEM((micro, shard, ff), BF16))

    def backward(GJ, DS):
        sJ = [
            ScatterZFirst(
                l,
                scatter_sems,
                5 + g,
                sums(SJ.at[g]),
                j_bufs[g],
                (lambda ref: lambda bz, by, bx: ref.at[c, bz, by, bx])(GJ.at[g]),
                over("sJ%d" % g),
            )
            for g in range(sets)
        ]
        firstJ = [
            Again(
                lambda g=g: remote(
                    GJ.at[g, 1 - c], SJ.at[g], first_sems, (4, g), l.sib
                )
            )
            for g in range(sets)
        ]
        items = dict(sR1=sR1, sR2=sR2, sE=sE, sO=sO, sV=sV)
        for g in range(sets):
            items["sJ%d" % g] = sJ[g]
        first = dict(sE=[firstE], sO=[firstO], sV=[firstV])
        for g in range(sets):
            first["sJ%d" % g] = [firstJ[g]]

        def run(order):
            for step in order:
                name, what = step.split(".")
                if what == "go":
                    for copy in dict(yex=y_ex, gx=far_ex)[name]:
                        copy.start()
                elif what == "add_sib":
                    items[name].add_sib(first[name])
                else:
                    getattr(items[name], what)()

        def back_norm(m, carry):
            grad = FX[m]
            normal = X1[m]
            GVEC[GAIN1 : GAIN1 + 1, :width] += jnp.sum(grad * normal, axis=0, keepdims=True)
            GVEC[SHIFT1 : SHIFT1 + 1, :width] += jnp.sum(grad, axis=0, keepdims=True)
            dn = grad * bias(GAIN1)
            grad = I1[m][:, :1] * (dn - rows_mean(dn) - normal * rows_mean(dn * normal))
            FX[m] = grad
            grad_low = grad.astype(BF16)
            DRED[m] = grad_low
            GVEC[OUTPUT_B : OUTPUT_B + 1, :width] += jnp.sum(
                grad_low.astype(F32), axis=0, keepdims=True
            )
            return carry

        steps(micro, back_norm)
        run(SCATTER_ORDER[0])

        def back_output():
            branch = lambda h: DRED[:, :, h * oh : (h + 1) * oh].reshape(own_rows, oh)
            attended_grad = dot_t(branch(0), wide(O, 0, 0, oh)) + dot_t(
                branch(1), wide(O, 1, 0, oh)
            )
            HL[...] = attended_grad.astype(BF16).reshape(HL.shape)
            for h in range(2):
                grad = t_dot(ATT[...].reshape(own_rows, width), branch(h))
                O[h] = grad.astype(BF16).reshape(O.shape[1:])

        once(back_output)
        firstO.start()
        run(SCATTER_ORDER[1])

        for g in range(sets):

            def back_attend(i, carry, g=g):
                q_at, k_at, v_at, o_at = pair_at(g, i)
                k = QKV[:, :, k_at].reshape(pack, 128)
                v = QKV[:, :, v_at].reshape(pack, 128)
                d_outs, queries, dqs = [], [], []
                for m in range(micro):
                    d_out = stacked(HL[m, :, o_at])
                    prob = PR[g, i, m].astype(F32)
                    product = prob * dot_t(d_out, v)
                    delta = jnp.sum(product, axis=-1, keepdims=True)
                    score_grad = (product - prob * delta).astype(BF16)
                    DS[m] = score_grad
                    dqs.append(unstacked(dot(score_grad, k)) * (HD ** (-0.5)))
                    d_outs.append(d_out)
                    queries.append(stacked(QKV[m, :, q_at]))
                dk = t_dot(DS[...].reshape(2 * pack, pack), jnp.concatenate(queries, axis=0))
                dv = t_dot(
                    PR[g, i].reshape(2 * pack, pack), jnp.concatenate(d_outs, axis=0)
                ).astype(BF16)
                cosine, sine = cos_t[...].reshape(pack, 128), sin_t[...].reshape(pack, 128)
                dq = turn(jnp.concatenate(dqs, axis=0), cosine, sine, -1.0).astype(BF16)
                dk = turn(dk, cosine, sine, -1.0).astype(BF16)
                for n, (at, grad) in enumerate(((q_at, dq), (k_at, dk), (v_at, dv))):
                    QKV[:, :, at] = grad.reshape(micro, shard, 128)
                    to = pl.ds(pl.multiple_of(n * width + g * part + i * 128, 128), 128)
                    GVEC[JOINT_B : JOINT_B + 1, to] = jnp.sum(
                        grad.astype(F32), axis=0, keepdims=True
                    )
                return carry

            steps(PAIRS, back_attend)
            run(SCATTER_ORDER[2 + 2 * g])

            set_grad = lambda: QKV[:, :, 3 * g * part : 3 * (g + 1) * part].reshape(
                own_rows, 3 * part
            )

            def joint_rows():
                grad = t_dot(T[...].reshape(own_rows, width), set_grad()).astype(BF16)
                GJ[g, 0] = grad[:, :hp].reshape(GJ.shape[2:])
                GJ[g, 1] = grad[:, hp:].reshape(GJ.shape[2:])

            def back_tokens():
                FX[...] += dot_t(set_grad(), set_weights(g)).reshape(FX.shape)

            once(joint_rows)
            firstJ[g].start()
            once(back_tokens)
            run(SCATTER_ORDER[3 + 2 * g])

        DRED[...] = FX[...].astype(BF16)
        keep_far.start()
        run(SCATTER_ORDER[2 + 2 * sets])
        pl.run_scoped(pack_grads, sel_shape)
        firstV.start()
        run(SCATTER_ORDER[3 + 2 * sets])

        def settle(item, stage, at=0):
            total = item.total()
            rows, columns = stage.shape[1], total.shape[1]
            stage[0, :, at : at + columns] = total[:rows]
            stage[1, :, at : at + columns] = total[rows:]

        def swap(n, stage, pair):
            copy = remote(stage.at[1 - c], pair, last_sems, n, l.sib)
            copy.start()
            return copy

        def both(copy, stage, pair):
            copy.wait_recv()
            mine = stage[c]
            other = pair[...]
            return jnp.where(c == 0, mine, other), jnp.where(c == 0, other, mine)

        gr[:split] = sR1.total()
        gr[split:] = sR2.total()
        ready["gr"].start()
        settle(sE, stage_e)
        lastE = swap(0, stage_e, pair_e)
        settle(sO, stage_o)
        lastO = swap(1, stage_o, pair_o)
        for copy, out, stage, pair in (
            (lastE, ge, stage_e, pair_e),
            (lastO, go, stage_o, pair_o),
        ):
            half = stage.shape[2]
            out[:, :half], out[:, half:] = both(copy, stage, pair)
        ready["ge"].start()
        ready["go"].start()
        run(SCATTER_ORDER[4 + 2 * sets])
        for g in range(sets):
            settle(sJ[g], stage_j, g * hp)
        lastJ = swap(2, stage_j, pair_j)
        left, right = both(lastJ, stage_j, pair_j)
        for g in range(sets):
            q, k, v = (n * width + g * part for n in range(3))
            at = g * hp
            gj[:, q : q + part] = left[:, at : at + part]
            gj[:, k : k + hp - part] = left[:, at + part : at + hp]
            gj[:, k + hp - part : k + part] = right[:, at : at + hp - part]
            gj[:, v : v + part] = right[:, at + hp - part : at + hp]
        ready["gj"].start()
        run(SCATTER_ORDER[5 + 2 * sets])
        gv[...] = sV.total()
        ready["gv"].start()
        for copy in y_ex + far_ex:
            copy.wait_recv()
        for copy in firstR + [firstO, firstV] + firstJ + y_ex + far_ex:
            copy.wait_send()
        for copy in (lastE, lastO, lastJ):
            copy.wait_send()
        for item in items.values():
            item.drain()
        keep_y.wait()
        keep_far.wait()
        for copy in ready.values():
            copy.wait()

    pl.run_scoped(
        backward, pltpu.VMEM(J.shape, BF16), pltpu.VMEM((micro, 2 * shard, pack), BF16)
    )


def layer(zs, lengths, weights, vectors, tok, cot):
    jw, ow, ew, rw = weights
    micro, shard, width = tok.shape
    vmem = pl.BlockSpec(memory_space=pltpu.VMEM)
    hbm = pl.BlockSpec(memory_space=pl.ANY)
    smem = pl.BlockSpec(memory_space=pltpu.SMEM)
    devices = zs * 8
    pack = micro * shard
    ff = devices * rw.shape[0]
    widths = [v.shape[0] for v in vectors]
    vectors = [v[None, :] for v in vectors]
    paired = (jw, ow, ew)
    sets = width // (128 * PAIRS)
    dma = pltpu.SemaphoreType.DMA

    def sems(*shape):
        return (dma(shape), dma(shape))

    def halves(w):
        return (2, zs, 2, 2, 2 * w.shape[0], w.shape[1] // 2)

    def reduction(shape, dtype=BF16):
        column = (zs,) + shape
        return (
            pltpu.VMEM(column, dtype),
            pltpu.VMEM(column, dtype),
            pltpu.VMEM(column, dtype),
            pltpu.VMEM((zs - 1,) + shape, dtype),
        )

    r1_block = (rw.shape[0] // 3, rw.shape[1])
    r2_block = (rw.shape[0] - r1_block[0], rw.shape[1])
    r2_bufs = (
        pltpu.VMEM(r2_block, BF16),
        pltpu.VMEM(r2_block, BF16),
        pltpu.VMEM(r2_block, BF16),
        pltpu.VMEM((zs - 1, 2, 2) + r2_block, BF16),
    )
    j_block = (2 * jw.shape[0], 3 * 128 * PAIRS // 2)
    rows = (micro, shard, width)
    scratch = (
        [pltpu.VMEM(w.shape, F32) for w in weights]
        + [pltpu.VMEM(VECTOR_TILE, F32)]
        + [pltpu.VMEM((sets, 2, zs, 2, 2, 2 * jw.shape[0], 3 * 128 * PAIRS // 2), BF16)]
        + [pltpu.VMEM(halves(w), BF16) for w in (ow, ew)]
        + [
            pltpu.VMEM((zs, 2, 2, 2) + rw.shape, BF16),
            pltpu.VMEM((zs, 2, 2, 2) + VECTOR_TILE, F32),
            pltpu.VMEM(rows, BF16),
        ]
        + [pltpu.VMEM((2, w.shape[0], w.shape[1] // 2), F32) for w in paired]
        + [pltpu.VMEM((w.shape[0], w.shape[1] // 2), F32) for w in paired]
        + [
            pltpu.VMEM((micro, shard, 128), F32),
            pltpu.VMEM((micro, shard, 128), F32),
            pltpu.VMEM((micro, shard, 3 * width), BF16),
            pltpu.VMEM((sets, PAIRS, micro, 2 * shard, pack), BF16),
            pltpu.VMEM(rows, BF16),
            pltpu.VMEM(rows, F32),
            pltpu.VMEM((micro, shard, 128), F32),
            pltpu.VMEM(rows, BF16),
            pltpu.VMEM(rows, F32),
            pltpu.VMEM(rows, BF16),
            pltpu.VMEM(rows, BF16),
            pltpu.VMEM((8, ff), F32),
            pltpu.VMEM((8, ff), F32),
            pltpu.VMEM((zs, 2, 2) + rw.shape, BF16),
        ]
        + [pltpu.VMEM(halves(w)[1:], BF16) for w in (ew, ow)]
        + [
            pltpu.VMEM((sets, zs, 2, 2) + j_block, BF16),
            pltpu.VMEM((zs, 2, 2) + VECTOR_TILE, F32),
            reduction(r1_block),
            r2_bufs,
        ]
        + [reduction(halves(w)[4:]) for w in (ew, ow)]
        + [
            [reduction(j_block) for _ in range(sets)],
            reduction(VECTOR_TILE, F32),
            pltpu.VMEM((zs, 2, 2, 2) + VECTOR_TILE, F32),
            sems(3),
            sems(6 + sets, zs + 6),
            sems(micro - 1),
            sems(micro - 1),
            sems(micro - 1),
            sems(micro - 1),
            sems(5, max(zs, sets)),
            sems(5 + sets, zs + 2),
            sems(3),
            dma((4,)),
            dma((5,)),
        ]
    )
    shapes = [
        jax.ShapeDtypeStruct(rows, BF16),
        jax.ShapeDtypeStruct(rows, BF16),
        jax.ShapeDtypeStruct(jw.shape, F32),
        jax.ShapeDtypeStruct(ow.shape, F32),
        jax.ShapeDtypeStruct(ew.shape, F32),
        jax.ShapeDtypeStruct(rw.shape, F32),
        jax.ShapeDtypeStruct(VECTOR_TILE, F32),
    ]
    return pl.pallas_call(
        functools.partial(layer_kernel, zs, widths),
        out_shape=shapes,
        in_specs=[smem] + [vmem] * 4 + [hbm] * 2 + [vmem] * 8,
        out_specs=[hbm] * 7,
        scratch_shapes=scratch,
        compiler_params=pltpu.CompilerParams(
            collective_id=0, has_side_effects=True, vmem_limit_bytes=64 << 20
        ),
    )(lengths, jw, ow, ew, rw, tok, cot, *vectors)


def deliver_kernel(widths, *refs):
    arrays, outs, held, more = refs[:7], refs[7:21], refs[21:28], refs[28:]
    wide, shares, (come, go) = more[0], more[1:9], more[9:]
    into = [
        pltpu.make_async_copy(array, hold, come.at[n])
        for n, (array, hold) in enumerate(zip(arrays, held))
    ]
    out = [
        pltpu.make_async_copy(hold, result, go.at[n])
        for n, (hold, result) in enumerate(zip((wide,) + held[1:6] + shares, outs))
    ]
    for copy in into:
        copy.start()
    into[0].wait()
    wide[...] = held[0][...].astype(F32)
    out[0].start()
    for n in range(1, 6):
        into[n].wait()
        out[n].start()
    into[6].wait()
    for i, share in enumerate(widths):
        shares[i][...] = held[6][i, :share]
        out[6 + i].start()
    for copy in out:
        copy.wait()


def deliver(widths, arrays):
    hbm = pl.BlockSpec(memory_space=pl.ANY)
    shares = [jax.ShapeDtypeStruct((w,), F32) for w in widths]
    wide = jax.ShapeDtypeStruct(arrays[0].shape, F32)
    return pl.pallas_call(
        functools.partial(deliver_kernel, widths),
        out_shape=[wide]
        + [jax.ShapeDtypeStruct(a.shape, a.dtype) for a in arrays[1:6]]
        + shares,
        in_specs=[hbm] * 7,
        out_specs=[hbm] * 14,
        scratch_shapes=[pltpu.VMEM(a.shape, a.dtype) for a in arrays]
        + [pltpu.VMEM(a.shape, a.dtype) for a in [wide] + shares]
        + [pltpu.SemaphoreType.DMA((7,)), pltpu.SemaphoreType.DMA((14,))],
        compiler_params=pltpu.CompilerParams(vmem_limit_bytes=62 << 20),
    )(*arrays)


def layout(lengths, places):
    doc_ends = jnp.cumsum(lengths)
    starts = doc_ends - lengths
    segment = jnp.sum((places[:, None] >= doc_ends[None, :]).astype(jnp.int32), axis=1)
    labels = jnp.arange(lengths.shape[0], dtype=jnp.int32)
    doc_begin = jnp.sum(jnp.where(segment[:, None] == labels[None, :], starts[None, :], 0), axis=1)
    doc_begin = jnp.where(segment == lengths.shape[0], doc_ends[-1], doc_begin)
    return (segment, places - doc_begin)


def rotate(entries, angles, direction):
    half_width = HD // 2
    cosine = jnp.cos(angles)[:, :, None, :]
    sine_part = direction * jnp.sin(angles)[:, :, None, :]
    pieces = entries.reshape(entries.shape[0], entries.shape[1], -1, HD)
    first_half = pieces[..., :half_width]
    second_half = pieces[..., half_width:]
    turned = jnp.concatenate(
        [
            first_half * cosine - second_half * sine_part,
            second_half * cosine + first_half * sine_part,
        ],
        axis=-1,
    )
    return turned.reshape(entries.shape)


def normalize(residual, gain_vector, offset):
    centered = residual - jnp.mean(residual, axis=-1, keepdims=True)
    inverse_std = lax.rsqrt(jnp.mean(centered * centered, axis=-1, keepdims=True) + EPSILON)
    return centered * inverse_std * gain_vector + offset


def contract_rows(left, right):
    return lax.dot_general(
        left, right, (((0,), (0,)), ((), ())), preferred_element_type=F32
    )


def times_transposed(left, right):
    return lax.dot_general(
        left, right, (((1,), (1,)), ((), ())), preferred_element_type=F32
    )


def column_sum(values):
    return jnp.sum(values.astype(F32), axis=0)


def per_device(
    mesh_shape,
    tokens,
    document_lengths,
    joint_weight,
    joint_bias,
    output_weight,
    output_bias,
    first_gain,
    first_shift,
    expand_weight,
    expand_bias,
    reduce_weight,
    reduce_bias,
    second_gain,
    second_shift,
    cotangent,
):
    dp_size, blk_size = mesh_shape
    micro, _, shard_rows, width = tokens.shape
    own = micro * shard_rows
    pack_rows = shard_rows * blk_size
    vectors = (
        joint_bias,
        output_bias,
        first_gain,
        first_shift,
        expand_bias,
        reduce_bias,
        second_gain,
        second_shift,
    )
    widths = [v.shape[0] for v in vectors]
    use_kernels = (
        blk_size == 4
        and micro == blk_size
        and dp_size == 8
        and (2 * joint_weight.shape[0]) % 16 == 0
        and reduce_weight.shape[0] % 48 == 0
    )
    zs = dp_size // 2
    axes = ("dp", "blk")
    tokens_own = tokens[:, 0]
    if use_kernels:
        y, far, gj, go, ge, gr, gv = layer(
            zs,
            document_lengths[:, 0],
            (joint_weight, output_weight, expand_weight, reduce_weight),
            vectors,
            tokens_own,
            cotangent[:, 0],
        )
        gx, y, gj, go, ge, gr, *shares = deliver(
            widths, (far, y, gj, go, ge, gr, gv)
        )
        return (y[:, None], gx[:, None], gj, shares[0], go) + tuple(shares[1:4]) + (
            ge,
            shares[4],
            gr,
        ) + tuple(shares[5:])
    joint_full, output_full, expand_full, reduce_full = (
        lax.all_gather(w, axes, axis=0, tiled=True)
        for w in (joint_weight, output_weight, expand_weight, reduce_weight)
    )
    packed = lax.all_gather(jnp.concatenate(vectors), axes, axis=0)
    cuts = [sum(widths[: i + 1]) for i in range(len(widths) - 1)]
    vector_full = [
        v.reshape(-1).astype(F32) for v in jnp.split(packed, cuts, axis=1)
    ]
    pack = lax.all_gather(tokens_own, "blk", axis=0)
    joint_b, output_b, gain1, shift1, expand_b, reduce_b, gain2, shift2 = vector_full

    pack_tokens = pack.transpose(1, 0, 2, 3).reshape(micro, pack_rows, width)
    lengths = document_lengths[:, 0]
    all_places = jnp.arange(pack_rows, dtype=jnp.int32)
    own_start = lax.axis_index("blk") * shard_rows
    key_segment, key_inner = jax.vmap(layout, (0, None))(lengths, all_places)
    segment = lax.dynamic_slice_in_dim(key_segment, own_start, shard_rows, 1)
    inner = lax.dynamic_slice_in_dim(key_inner, own_start, shard_rows, 1)
    frequency = 10000.0 ** (-jnp.arange(HD // 2, dtype=F32) * (2.0 / HD))
    key_angles = key_inner.astype(F32)[..., None] * frequency
    query_angles = inner.astype(F32)[..., None] * frequency
    score_scale = HD ** (-0.5)

    token_low = tokens_own.reshape(own, width)
    token_float = token_low.astype(F32)
    query_weight, pair_weight = joint_full[:, :width], joint_full[:, width:]
    query = jnp.dot(token_low, query_weight, preferred_element_type=F32) + joint_b[:width]
    query = rotate(query.reshape(micro, shard_rows, width), query_angles, 1.0).astype(BF16)
    pair = (
        jnp.dot(
            pack_tokens.reshape(micro * pack_rows, width),
            pair_weight,
            preferred_element_type=F32,
        )
        + joint_b[width:]
    ).reshape(micro, pack_rows, 2 * width)
    keys = rotate(pair[..., :width], key_angles, 1.0).astype(BF16)
    values = pair[..., width:].astype(BF16)
    query_heads = query.reshape(micro, shard_rows, H, HD)
    key_heads = keys.reshape(micro, pack_rows, H, HD)
    value_heads = values.reshape(micro, pack_rows, H, HD)
    allowed = (segment[:, :, None] == key_segment[:, None, :])[:, None]
    scores = (
        jnp.einsum("mqhd,mkhd->mhqk", query_heads, key_heads, preferred_element_type=F32)
        * score_scale
    )
    scores = jnp.where(allowed, scores, NEGATIVE)
    highest = jnp.max(scores, axis=-1, keepdims=True)
    weights = jnp.where(allowed, jnp.exp(scores - highest), 0.0)
    probability = weights / jnp.sum(weights, axis=-1, keepdims=True)
    probability_low = probability.astype(BF16)
    attended = (
        jnp.einsum("mhqk,mkhd->mqhd", probability_low, value_heads, preferred_element_type=F32)
        .reshape(own, width)
        .astype(BF16)
    )
    branch = jnp.dot(attended, output_full, preferred_element_type=F32) + output_b
    hidden, first_pullback = jax.vjp(normalize, token_float + branch, gain1, shift1)
    hidden_low = hidden.astype(BF16)
    expanded = jnp.dot(hidden_low, expand_full, preferred_element_type=F32) + expand_b
    active_float, gelu_pullback = jax.vjp(jax.nn.gelu, expanded)
    active = active_float.astype(BF16)
    reduced = jnp.dot(active, reduce_full, preferred_element_type=F32) + reduce_b
    result, second_pullback = jax.vjp(normalize, hidden + reduced, gain2, shift2)
    layer_output = result.astype(BF16).reshape(tokens.shape)

    second_residual, second_gain_grad, second_shift_grad = second_pullback(
        cotangent[:, 0].reshape(own, width).astype(F32)
    )
    reduced_grad = second_residual.astype(BF16)
    reduce_weight_grad = contract_rows(active, reduced_grad)
    reduce_bias_grad = column_sum(reduced_grad)
    (expanded_float,) = gelu_pullback(times_transposed(reduced_grad, reduce_full))
    expanded_grad = expanded_float.astype(BF16)
    expand_bias_grad = column_sum(expanded_grad)
    hidden_grad = second_residual + times_transposed(expanded_grad, expand_full)
    first_residual, first_gain_grad, first_shift_grad = first_pullback(hidden_grad)
    branch_grad = first_residual.astype(BF16)
    output_bias_grad = column_sum(branch_grad)
    attended_grad = times_transposed(branch_grad, output_full).astype(BF16)
    attended_heads = attended_grad.reshape(micro, shard_rows, H, HD)
    prob_grad = jnp.einsum(
        "mqhd,mkhd->mhqk", attended_heads, value_heads, preferred_element_type=F32
    )
    delta = jnp.sum(probability * prob_grad, axis=-1, keepdims=True)
    score_grad = (probability * (prob_grad - delta)).astype(BF16)
    query_grad = (
        jnp.einsum("mhqk,mkhd->mqhd", score_grad, key_heads, preferred_element_type=F32)
        * score_scale
    ).reshape(micro, shard_rows, width)
    key_grad = (
        jnp.einsum("mhqk,mqhd->mkhd", score_grad, query_heads, preferred_element_type=F32)
        * score_scale
    ).reshape(micro, pack_rows, width)
    value_grad = jnp.einsum(
        "mhqk,mqhd->mkhd", probability_low, attended_heads, preferred_element_type=F32
    ).reshape(micro, pack_rows, width)
    query_back = rotate(query_grad, query_angles, -1.0).reshape(own, width).astype(BF16)
    key_back = rotate(key_grad, key_angles, -1.0)
    pair_back = (
        jnp.concatenate([key_back, value_grad], axis=-1)
        .astype(BF16)
        .reshape(micro * pack_rows, 2 * width)
    )
    joint_bias_grad = jnp.concatenate([column_sum(query_back), column_sum(pair_back)])
    pack_flat = pack_tokens.reshape(micro * pack_rows, width)
    near_gradient = first_residual + times_transposed(query_back, query_weight)
    far_gradient = (
        times_transposed(pair_back, pair_weight)
        .astype(BF16)
        .reshape(micro, blk_size, shard_rows, width)
        .transpose(1, 0, 2, 3)
    )
    near_gradient = near_gradient.reshape(tokens_own.shape)
    vector_grads = (
        joint_bias_grad,
        output_bias_grad,
        first_gain_grad,
        first_shift_grad,
        expand_bias_grad,
        reduce_bias_grad,
        second_gain_grad,
        second_shift_grad,
    )
    joint_grad = jnp.concatenate(
        [contract_rows(token_low, query_back), contract_rows(pack_flat, pair_back)], axis=1
    )
    output_grad = contract_rows(attended, branch_grad)
    expand_grad = contract_rows(hidden_low, expanded_grad)
    gj, go, ge, gr = (
        lax.psum_scatter(g, axes, scatter_dimension=0, tiled=True)
        for g in (joint_grad, output_grad, expand_grad, reduce_weight_grad)
    )
    devices = dp_size * blk_size
    packed = jnp.concatenate([v.reshape(devices, -1) for v in vector_grads], axis=1)
    summed = lax.psum_scatter(packed, axes, scatter_dimension=0, tiled=True)
    cuts = [sum(widths[: i + 1]) for i in range(len(widths) - 1)]
    shares = [v.reshape(-1) for v in jnp.split(summed, cuts, axis=1)]
    far = lax.psum_scatter(far_gradient, "blk", scatter_dimension=0, tiled=True)
    input_gradient = near_gradient + far[0].astype(F32)
    return (
        layer_output,
        input_gradient[:, None],
        gj,
        shares[0],
        go,
        shares[1],
        shares[2],
        shares[3],
        ge,
        shares[4],
        gr,
        shares[5],
        shares[6],
        shares[7],
    )


def solution(mesh):
    rows = P(("dp", "blk"), None)
    row = P(("dp", "blk"))
    packs = P(None, "dp", "blk", None)
    parameters = (rows, row, rows, row, row, row, rows, row, rows, row, row, row)
    return jax.shard_map(
        functools.partial(per_device, (mesh.shape["dp"], mesh.shape["blk"])),
        mesh=mesh,
        in_specs=(packs, P(None, "dp", None)) + parameters + (packs,),
        out_specs=(packs, packs) + parameters,
        check_vma=False,
    )
```
